256 devices in a mesh: row: 4 (over x), col: 64 (over z, y, core).
Axes of the slice: x: 4, y: 4, z: 8, core: 2. Of those that a mesh axis runs over, the one named last changes fastest.
Arguments:
- sigma_trail: float32 [16384, 16384], P('row', 'col'), as said below
- panel_one: float32 [16384, 256], P(('row', 'col')), may hold values from -0.046875 to 0.046875
- panel_zero: float32 [16384, 256], P(('row', 'col')), may hold values from -0.046875 to 0.046875
- link: float32 [256, 256], replicated, may hold values from -0.375 to 0.375
- diag_one: float32 [256, 256], replicated, as said below
- diag_zero: float32 [256, 256], replicated, as said below
Outputs:
- sigma_s1: float32 [16384, 256], P(('row', 'col'))
- sigma_11: float32 [256, 256], replicated
- sigma_s0: float32 [16384, 256], P(('row', 'col'))
- sigma_10: float32 [256, 256], replicated
- sigma_00: float32 [256, 256], replicated
The draws below stay inside these ranges and needn't reach their ends.
Inputs may be any that keep to these rules, and one draw needn't show every extreme that they name: `sigma_trail`: symmetric once its rows and columns are both put back in the global order. `diag_one`: lower triangular, diagonal entries between 1 and 2. `diag_zero`: lower triangular, diagonal entries between 1 and 2.
All inputs are finite; a program needn't handle non-finite values.
Results may differ from the reference program's by a relative error of at most 0.000075.
Values sent between devices are 32-bit elements; how exact they have to be, the bound alone decides.
No kernel may reach another device: no remote copies, remote signals or barrier semaphores. Data moves between devices by JAX's collectives and lax.ppermute only.
A program may use at most 64 MiB of HBM per device.

```python
import jax
import jax.numpy as jnp
from jax import lax

B = 256
M = 16384
N_ROW = 4
N_COL = 64


def global_rows(grid_count):
    tiles = M // B
    places = jnp.arange(M, dtype=jnp.int32)
    tile_place = places // B
    offset = places % B
    owner = tile_place // (tiles // grid_count)
    within = tile_place % (tiles // grid_count)
    return ((within * grid_count + owner) * B + offset).astype(jnp.int32)


def triangle(key):
    key_fill, key_diag = jax.random.split(key)
    fill = jax.random.normal(key_fill, (B, B), jnp.float32) * (0.5 / B ** 0.5)
    diagonal = jax.random.uniform(key_diag, (B,), jnp.float32, 1.0, 2.0)
    return jnp.tril(fill, -1) + jnp.diag(diagonal)


def draw_sigma_trail(key, part):
    key = jax.random.fold_in(key, 11)
    key_scale, key_noise, key_diag = jax.random.split(key, 3)
    scales = jnp.exp(jax.random.uniform(key_scale, (M,), jnp.float32, -0.58, 0.58))
    noise = jax.random.normal(key_noise, (M, M), jnp.float32)
    symmetric = (noise + noise.T) * 0.7071
    diagonal = jax.random.uniform(key_diag, (M,), jnp.float32, 1.0, 4.0)
    whole = scales[:, None] * symmetric * scales[None, :] + jnp.diag(diagonal)
    whole = jnp.take(whole, global_rows(N_ROW), axis=0)
    return jnp.take(whole, global_rows(N_COL), axis=1)


def draw_diag_one(key, part):
    key = jax.random.fold_in(key, 21)
    return triangle(key)


def draw_diag_zero(key, part):
    key = jax.random.fold_in(key, 22)
    return triangle(key)


def shard_levels(rng, dims, shards, least, top_value):
    factor_of, own = 1.0, jax.random.fold_in(rng, 6)
    for position, blocks in shards:
        steps = jnp.exp(jax.random.uniform(jax.random.fold_in(own, position), (blocks,), jnp.float32, least / len(shards), top_value / len(shards)))
        factor_of = factor_of * jnp.repeat(steps, dims[position] // blocks).reshape([-1 if axis == position else 1 for axis in range(len(dims))])
    return factor_of


def gaussian(own_key, extent, deviation, reach, shards=(), held_as=jnp.bfloat16):
    drawn = deviation * jax.random.normal(own_key, extent, jnp.float32)
    if shards:
        drawn = drawn * shard_levels(own_key, extent, shards, -0.22, 0.18)
    return jnp.clip(drawn, -reach, reach).astype(held_as)


def setup_inputs(seed: int = 0) -> dict:
    splits = jax.random.split(jax.random.key(seed), 7)
    return {
        "sigma_trail": draw_sigma_trail(jax.random.fold_in(splits[6], 71), 0),
        "panel_one": gaussian(splits[1], (M, B), M ** -0.5, 0.046875, ((0, 256),), jnp.float32),
        "panel_zero": gaussian(splits[2], (M, B), M ** -0.5, 0.046875, ((0, 256),), jnp.float32),
        "link": gaussian(splits[3], (B, B), B ** -0.5, 0.375, (), jnp.float32),
        "diag_one": draw_diag_one(jax.random.fold_in(splits[6], 71), 0),
        "diag_zero": draw_diag_zero(jax.random.fold_in(splits[6], 71), 0),
    }


def matmul(left, right):
    return jnp.dot(left.astype(jnp.float32), right.astype(jnp.float32), precision=lax.Precision.HIGHEST, preferred_element_type=jnp.float32)

def normalize(panel, factor):
    return lax.linalg.triangular_solve(factor, panel, left_side=False, lower=True)

def inverse_block(factor):
    size_here = factor.shape[0]
    inverse = lax.linalg.triangular_solve(factor, jnp.eye(size_here, dtype=jnp.float32), left_side=True, lower=True)
    return matmul(inverse.T, inverse)

def column_rows(hat):
    tiles = M // B
    places = jnp.arange(tiles, dtype=jnp.int32)
    owner = places // (tiles // N_COL)
    within = places % (tiles // N_COL)
    global_tile = within * N_COL + owner
    row_place = global_tile % N_ROW * (tiles // N_ROW) + global_tile // N_ROW
    blocks = hat.reshape(tiles, B, hat.shape[1])
    return jnp.take(blocks, row_place.astype(jnp.int32), axis=0).reshape(M, hat.shape[1])

def reference(sigma_trail, panel_one, panel_zero, link, diag_one, diag_zero):
    hat_one = normalize(panel_one, diag_one)
    hat_zero = normalize(panel_zero, diag_zero)
    hat_link = normalize(link, diag_zero)
    sigma_s1 = -matmul(sigma_trail, column_rows(hat_one))
    sigma_11 = inverse_block(diag_one) - matmul(hat_one.T, sigma_s1)
    sigma_s0 = -(matmul(sigma_s1, hat_link) + matmul(sigma_trail, column_rows(hat_zero)))
    sigma_10 = -(matmul(sigma_11, hat_link) + matmul(sigma_s1.T, hat_zero))
    sigma_00 = inverse_block(diag_zero) - matmul(hat_link.T, sigma_10) - matmul(hat_zero.T, sigma_s0)
    return (sigma_s1, sigma_11, sigma_s0, sigma_10, sigma_00)
```

```python
import jax
import jax.numpy as jnp
from jax import lax
from jax.experimental import pallas as pl
from jax.experimental.pallas import tpu as pltpu
from jax.sharding import Mesh, PartitionSpec as P

F32 = jnp.float32
BF16 = jnp.bfloat16
AXES = ("x", "z", "y", "s")
NX, NY, NZ = 4, 4, 8
B = 256
Q = 64
HALF = 128


def device(x, y, z, s):
    return (x % NX) * 64 + (z % NZ) * 8 + (y % NY) * 2 + s


def send(block, move):
    pairs = [
        (device(x, y, z, s), device(*move(x, y, z, s)))
        for x in range(NX)
        for z in range(NZ)
        for y in range(NY)
        for s in range(2)
    ]
    return lax.ppermute(block, AXES, pairs)


def to_core(block):
    return send(block, lambda x, y, z, s: (x, y, z, 1 - s))


def along_y(block):
    return send(block, lambda x, y, z, s: (x, y + 1 - 2 * s, z, s))


def along_z(block):
    return send(block, lambda x, y, z, s: (x, y, z + 1 - 2 * s, s))


SLOTS = ((0, 3, 1, 2), (0, 1, 3, 2))


def swap(block, axis, turn):
    def move(x, y, z, s):
        apart = SLOTS[s][2 - turn]
        return (x ^ apart, y, z, s) if axis == "x" else (x, y ^ apart, z, s)

    return send(block, move)


def gather_four(piece, axis):
    def far(d):
        return send(piece, lambda x, y, z, s: (x ^ d, y, z, s) if axis == "x" else (x, y ^ d, z, s))

    return jnp.stack([piece, far(1), far(2), far(3)])


def after(value, *earlier):
    return lax.optimization_barrier((value, earlier))[0]


def split(value):
    high = value.astype(BF16)
    return high, (value - high.astype(F32)).astype(BF16)


def dot3(left, right, dims):
    lh, ll = split(left)
    rh, rl = split(right)
    d = (dims, ((), ()))
    out = lax.dot_general(lh, rh, d, preferred_element_type=F32)
    out += lax.dot_general(ll, rh, d, preferred_element_type=F32)
    return out + lax.dot_general(lh, rl, d, preferred_element_type=F32)


NN = ((1,), (0,))
TN = ((0,), (0,))


def fill_left(ref, row, place, value):
    deep = ref.shape[1] // 3
    high, low = split(value)
    m, k = value.shape
    ref[row : row + m, place : place + k] = high
    ref[row : row + m, deep + place : deep + place + k] = low
    ref[row : row + m, 2 * deep + place : 2 * deep + place + k] = high


def fill_right(ref, place, column, value):
    deep = ref.shape[0] // 3
    high, low = split(value)
    k, n = value.shape
    ref[place : place + k, column : column + n] = high
    ref[deep + place : deep + place + k, column : column + n] = high
    ref[2 * deep + place : 2 * deep + place + k, column : column + n] = low


def product(left, right):
    return jnp.dot(left, right, preferred_element_type=F32)


def exact(left, right):
    return jnp.dot(left, right, precision=lax.Precision.HIGHEST, preferred_element_type=F32)


def params(limit=16):
    return pltpu.CompilerParams(vmem_limit_bytes=limit * 1024 * 1024)


def cost(flops, moved):
    return pl.CostEstimate(flops=flops, bytes_accessed=moved, transcendentals=0)


VMEM = pl.BlockSpec(memory_space=pltpu.VMEM)
SMEM = pl.BlockSpec(memory_space=pltpu.SMEM)
HBM = pl.BlockSpec(memory_space=pltpu.HBM)
WIDE = 6 * B
SLAB = (NY, 2, Q, B)


def slab_product(at, step, own, other, even, odd, left, right, slabs, sems):
    y, s, slab = at[1], at[3], at[4 + step]
    copies = [
        pltpu.make_async_copy(ref.at[slab], slabs.at[n], sems.at[n]) for n, ref in enumerate((own, other))
    ]
    for copy in copies:
        copy.start()
    depth = even.shape[0] * Q
    for n, ref in enumerate((even, odd)):
        for panel in range(2):
            fill_right(right, n * depth, panel * B, ref[:, panel].reshape(depth, B))
    near = lax.rem(y + 3 + 2 * s, NY)
    for o in range(2):
        copies[o].wait()
        for n, first in enumerate((y, near)):
            blocks = [
                slabs[o, lax.rem(first + 2 * d, NY), core]
                for d in range(2)
                for core in (s, 1 - s)[: depth // 128]
            ]
            fill_left(left, o * B, n * depth, jnp.concatenate(blocks, axis=0).T)
    return product(left[...], right[...])


def slab_scratch(even):
    deep = 6 * even.shape[0] * Q
    return [
        pltpu.VMEM((2 * B, deep), BF16),
        pltpu.VMEM((deep, 2 * B), BF16),
        pltpu.VMEM((2,) + SLAB, F32),
        pltpu.SemaphoreType.DMA((2,)),
    ]


def multiply(place, step, sigma, other, even, odd, total=None):
    totals = [] if total is None else [total]

    def kernel(at, own_ref, other_ref, even_ref, odd_ref, *refs):
        s = at[3]
        out = refs[len(totals)]
        value = slab_product(at, step, own_ref, other_ref, even_ref, odd_ref, *refs[len(totals) + 1 :])
        for o, tile in enumerate((s, 1 - s)):
            part = value[o * B : (o + 1) * B]
            out[tile] = part if total is None else part + refs[0][tile]

    return pl.pallas_call(
        kernel,
        in_specs=[SMEM, HBM, HBM] + [VMEM] * (2 + len(totals)),
        out_specs=VMEM,
        out_shape=jax.ShapeDtypeStruct((2, B, 2 * B), F32),
        scratch_shapes=slab_scratch(even),
        input_output_aliases={5: 0} if totals else {},
        compiler_params=params(30),
        cost_estimate=cost(3 << 28, 2 << 20),
        name="multiply",
    )(place, sigma, other, even, odd, *totals)


N = 3 * B // 32


def last_kernel(at, own, other, even, odd, total, weights, pieces, whole, t_all, t_right, *scratch):
    x, y, s = at[2], at[1], at[3]
    value = slab_product(at, 4, own, other, even, odd, *scratch)
    for o, tile in enumerate((s, 1 - s)):
        t_all[tile] = total[tile] + value[o * B : (o + 1) * B]
    fill_right(t_right, 0, 0, t_all[...].reshape(2 * B, 2 * B))
    top = product(weights[:B], t_right[...])
    whole[:B] = top[:, :B]
    whole[B : 2 * B] = top[:, B:]
    whole[2 * B :] = product(weights[B:], t_right[:, B:])
    for core in range(2):
        for slot, apart in enumerate(SLOTS[core]):
            p = x ^ apart
            for sub, further in enumerate(SLOTS[core]):
                start = (core * NX + p) * (NY * N) + (y ^ further) * N
                pieces[core ^ s, slot, sub * N : (sub + 1) * N] = whole[pl.ds(pl.multiple_of(start, 8), N), :]
            rows = pl.ds(pl.multiple_of((p // 2 * 2 + core) * Q, 8), Q)
            for panel in range(2):
                start = NY * N + panel * Q
                pieces[core ^ s, slot, start : start + Q] = t_all[lax.rem(p, 2), rows, panel * B : (panel + 1) * B]


def last(place, sigma, other, even, odd, total, weights):
    return pl.pallas_call(
        last_kernel,
        in_specs=[SMEM, HBM, HBM] + [VMEM] * 4,
        out_specs=VMEM,
        out_shape=jax.ShapeDtypeStruct((2, NX, NY * N + 2 * Q, B), F32),
        scratch_shapes=[
            pltpu.VMEM((3 * B, B), F32),
            pltpu.VMEM((2, B, 2 * B), F32),
            pltpu.VMEM((WIDE, 2 * B), BF16),
        ]
        + slab_scratch(even),
        compiler_params=params(30),
        cost_estimate=cost(1 << 30, 2 << 20),
        name="last",
    )(place, sigma, other, even, odd, total, weights)


def invert_kernel(_, one_ref, zero_ref, out_one, out_zero, one, zero, sems):
    copies = [pltpu.make_async_copy(one_ref, one, sems.at[0]), pltpu.make_async_copy(zero_ref, zero, sems.at[1])]
    for copy in copies:
        copy.start()
    for copy in copies:
        copy.wait()
    row = lax.broadcasted_iota(jnp.int32, (HALF, HALF), 0)
    col = lax.broadcasted_iota(jnp.int32, (HALF, HALF), 1)
    blocks, inverses = [], []
    for ref in (one, zero):
        for k in range(2):
            block = ref[k * HALF : (k + 1) * HALF, k * HALF : (k + 1) * HALF]
            blocks.append(block)
            inverses.append(jnp.where(row == col, 1.0 / block, 0.0))
    below = jnp.logical_and(row == col + 1, row % 2 == 1)
    scales = [jnp.sum(i, axis=1, keepdims=True) for i in inverses]
    inverses = [
        i - r * jnp.where(below, b, 0.0) * jnp.sum(i, axis=0, keepdims=True)
        for b, i, r in zip(blocks, inverses, scales)
    ]
    size = 2
    while size < HALF:
        below = jnp.logical_and(
            row // (2 * size) == col // (2 * size),
            jnp.logical_and((row // size) % 2 == 1, (col // size) % 2 == 0),
        )
        middles = [exact(jnp.where(below, b, 0.0), i) for b, i in zip(blocks, inverses)]
        inverses = [i - exact(i, m) for i, m in zip(inverses, middles)]
        size *= 2
    for n, (ref, out) in enumerate(((one, out_one), (zero, out_zero))):
        top, bottom = inverses[2 * n], inverses[2 * n + 1]
        out[:HALF, :HALF] = top
        out[HALF:, HALF:] = bottom
        out[:HALF, HALF:] = jnp.zeros((HALF, HALF), F32)
        out[HALF:, :HALF] = -exact(bottom, exact(ref[HALF:, :HALF], top))


def invert(place, one, zero):
    tile = jax.ShapeDtypeStruct((B, B), F32)
    return pl.pallas_call(
        invert_kernel,
        in_specs=[SMEM, HBM, HBM],
        out_specs=[VMEM, VMEM],
        out_shape=[tile, tile],
        scratch_shapes=[pltpu.VMEM((B, B), F32), pltpu.VMEM((B, B), F32), pltpu.SemaphoreType.DMA((2,))],
        compiler_params=params(),
        cost_estimate=cost(1 << 32, 1 << 20),
        name="invert",
    )(place, one, zero)


def constants_kernel(x1_ref, x0_ref, link, z_terms, zt_terms, base):
    x1, x0 = x1_ref[...], x0_ref[...]
    hl = dot3(link[...], x0, NN)
    top = -dot3(x1, hl, NN)
    none = jnp.zeros((B, B), F32)
    for row, column, block in ((0, 0, x1), (0, B, top), (B, 0, none), (B, B, x0)):
        fill_right(z_terms, row, column, block)
        fill_left(zt_terms, column, row, block.T)
    inv1 = dot3(x1, x1, TN)
    cross = dot3(inv1, hl, NN)
    base[:B] = inv1
    base[B : 2 * B] = -cross
    base[2 * B :] = dot3(x0, x0, TN) + dot3(hl, cross, TN)


def constants(x1, x0, link):
    return pl.pallas_call(
        constants_kernel,
        in_specs=[VMEM] * 3,
        out_specs=[VMEM] * 3,
        out_shape=[
            jax.ShapeDtypeStruct((WIDE, 2 * B), BF16),
            jax.ShapeDtypeStruct((2 * B, WIDE), BF16),
            jax.ShapeDtypeStruct((3 * B, B), F32),
        ],
        compiler_params=params(),
        cost_estimate=cost(1 << 29, 3 << 20),
        name="constants",
    )(x1, x0, link)


def weigh_kernel(at, mine, others, weights, rows):
    x, y, s = at[2], at[1], at[3]
    for tile in range(2):
        for g in range(2):
            for core in range(2):
                near = (tile ^ lax.rem(x, 2)) * 2 + (g ^ lax.rem(y, 2))
                start = ((tile * 2 + g) * 2 + core) * Q
                for panel in range(2):
                    block = jnp.where(s == core, mine[near, panel], others[near, panel])
                    rows[start : start + Q, panel * B : (panel + 1) * B] = block
    fill_left(weights, 0, 0, rows[...].T)


def weigh(place, mine, others):
    return pl.pallas_call(
        weigh_kernel,
        in_specs=[SMEM] + [VMEM] * 2,
        out_specs=VMEM,
        out_shape=jax.ShapeDtypeStruct((2 * B, WIDE), BF16),
        scratch_shapes=[pltpu.VMEM((2 * B, 2 * B), F32)],
        compiler_params=params(),
        cost_estimate=cost(1 << 28, 3 << 20),
        name="weigh",
    )(place, mine, others)


def rows_kernel(a, b, z_terms, sigmas, left):
    for panel in range(2):
        rows = slice(NY * N + panel * Q, NY * N + (panel + 1) * Q)
        fill_left(left, 0, panel * B, a[rows] + b[rows])
    both = product(left[...], z_terms[...])
    sigmas[0] = -both[:, :B]
    sigmas[1] = -both[:, B:]


def rows(a, b, z_terms):
    return pl.pallas_call(
        rows_kernel,
        in_specs=[VMEM] * 3,
        out_specs=VMEM,
        out_shape=jax.ShapeDtypeStruct((2, Q, B), F32),
        scratch_shapes=[pltpu.VMEM((Q, WIDE), BF16)],
        compiler_params=params(),
        cost_estimate=cost(1 << 27, 2 << 20),
        name="rows",
    )(a, b, z_terms)


def finish_kernel(at, mine, other, z_terms, zt_terms, base, s11, s10, s00, whole, left, right):
    x, y, s = at[2], at[1], at[3]
    for core in range(2):

        def place_all(ref):
            for slot, apart in enumerate(SLOTS[core]):
                for b in range(NY):
                    start = (core * NX + (x ^ apart)) * (NY * N) + (y ^ b) * N
                    whole[pl.ds(pl.multiple_of(start, 8), N), :] = ref[slot, b]

        @pl.when(s == core)
        def _():
            place_all(mine)

        @pl.when(s != core)
        def _():
            place_all(other)

    crossed = whole[B : 2 * B]
    fill_left(left, 0, 0, whole[:B])
    fill_left(left, 0, B, crossed)
    fill_left(left, B, 0, crossed.T)
    fill_left(left, B, B, whole[2 * B :])
    fill_right(right, 0, 0, product(left[...], z_terms[...]))
    top = product(zt_terms[:B], right[...])
    s11[...] = top[:, :B] + base[:B]
    s10[...] = top[:, B:] + base[B : 2 * B]
    s00[...] = product(zt_terms[B:], right[:, B:]) + base[2 * B :]


def finish(place, mine, other, z_terms, zt_terms, base):
    tile = jax.ShapeDtypeStruct((B, B), F32)
    return pl.pallas_call(
        finish_kernel,
        in_specs=[SMEM] + [VMEM] * 5,
        out_specs=[VMEM] * 3,
        out_shape=[tile, tile, tile],
        scratch_shapes=[
            pltpu.VMEM((3 * B, B), F32),
            pltpu.VMEM((2 * B, WIDE), BF16),
            pltpu.VMEM((WIDE, 2 * B), BF16),
        ],
        compiler_params=params(),
        cost_estimate=cost(1 << 28, 3 << 20),
        name="finish",
    )(place, mine, other, z_terms, zt_terms, base)


def body(sigma, p1, p0, link, diag_one, diag_zero):
    x, y, z, s = (lax.axis_index(name).astype(jnp.int32) for name in ("x", "y", "z", "s"))
    way = 2 * s - 1
    place = jnp.stack([z, y, x, s] + [lax.rem(z + NZ + j * way, NZ) for j in range(5)])

    view = (NZ,) + SLAB
    own = jnp.stack([p1, p0])[None]
    a = jnp.concatenate([own, to_core(own)], axis=0)
    y2 = send(own, lambda x, y, z, s: (x, y + 2, z, s))
    a1 = along_z(a)
    b = jnp.concatenate([after(y2, a), to_core(y2)], axis=0)
    b1 = along_z(b)
    a2 = along_z(after(a1, b))

    sigma_other = to_core(after(sigma, b, a1)).reshape(view)
    sigma = sigma.reshape(view)
    even = jnp.concatenate([own, after(y2, a1)], axis=0)
    odd = along_y(even)
    b1, odd = after((b1, odd), b1, odd)
    b2 = along_z(b1)
    z1 = jnp.concatenate([a1, b1], axis=0)
    e1 = along_y(z1)
    pair = jnp.concatenate([own, jnp.where(y % 2 == s, odd[1:], odd[:1])], axis=0)
    a3 = along_z(after(a2, b1))
    crossed = send(after(pair, a2), lambda x, y, z, s: (x ^ 2, y, z, s))
    total = multiply(place, 0, sigma, sigma_other, even, odd)

    b2 = after(b2, total, a2)
    b3 = along_z(b2)
    z2 = jnp.concatenate([a2, b2], axis=0)
    e2 = along_y(z2)
    a3 = after(a3, b2)
    first = jnp.where(x // 2 == y % 2, pair, after(crossed, b2))
    second = send(first, lambda x, y, z, s: (x ^ 1, y, z, s))
    total = multiply(place, 1, sigma, sigma_other, z1, e1, total)

    b3 = after(b3, total, a3)
    z4 = along_z(jnp.concatenate([a3[:1], b3[:1]], axis=0))
    z3 = jnp.concatenate([a3, b3], axis=0)
    e3 = along_y(z3)
    mine = jnp.concatenate([first, after(second, b3)], axis=0)
    others = to_core(mine)
    total = multiply(place, 2, sigma, sigma_other, z2, e2, total)
    weights = weigh(place, mine, others)

    z4 = after(z4, total, weights)
    e4 = along_y(z4)
    total = multiply(place, 3, sigma, sigma_other, z3, e3, total)
    pieces = last(place, sigma, sigma_other, z4, e4, total, weights)

    part = pieces[0] + to_core(pieces[1])
    came = swap(part[2:], "x", 0)
    x1, x0 = invert(after(place, part), diag_one, diag_zero)
    part = part[:2] + after(came, x1, x0)
    came = swap(part[1], "x", 1)
    z_terms, zt_terms, base = constants(x1, x0, after(link, part))
    parts = (part[0], after(came, base))
    part = (parts[0][: NY * N] + parts[1][: NY * N]).reshape(NY, N, B)
    sigmas = rows(*parts, z_terms)

    part = part[:2] + swap(part[2:], "y", 0)
    part = after(part, sigmas)
    part = part[0] + swap(part[1], "y", 1)
    part = part + send(part, lambda x, y, z, s: (x, y, z ^ 1, s))
    a, b, c = (send(part, lambda x, y, z, s: (x, y, z ^ far, s)) for far in (2, 4, 6))
    part = (part + a) + (b + c)
    sigmas = send(sigmas, lambda x, y, z, s: (y % 2 * 2 + x % 2, y // 2 * 2 + x // 2, z, s))
    mine = gather_four(part, "y")
    pair = jnp.stack([mine, swap(mine, "x", 1)])
    mine = after(jnp.concatenate([pair, swap(pair, "x", 0)], axis=0), sigmas)
    s11, s10, s00 = finish(place, mine, to_core(mine), z_terms, zt_terms, base)
    return sigmas[0], s11, sigmas[1], s10, s00


def solution(mesh):
    mesh = Mesh(mesh.devices.reshape(NX, NZ, NY, 2), AXES)
    in_specs = (P("x", AXES[1:]), P(AXES, None), P(AXES, None), P(), P(), P())
    out_specs = (P(AXES, None), P(), P(AXES, None), P(), P())
    return jax.shard_map(body, mesh=mesh, in_specs=in_specs, out_specs=out_specs, check_vma=False)
```

```python
import jax
import jax.numpy as jnp
from jax import lax
from jax.experimental import pallas as pl
from jax.experimental.pallas import tpu as pltpu
from jax.sharding import Mesh, PartitionSpec as P

F32 = jnp.float32
BF16 = jnp.bfloat16
AXES = ("x", "z", "y", "s")
NX, NY, NZ = 4, 4, 8
B = 256
Q = 64
HALF = 128


def device(x, y, z, s):
    return (x % NX) * 64 + (z % NZ) * 8 + (y % NY) * 2 + s


def send(block, move):
    pairs = [
        (device(x, y, z, s), device(*move(x, y, z, s)))
        for x in range(NX)
        for z in range(NZ)
        for y in range(NY)
        for s in range(2)
    ]
    return lax.ppermute(block, AXES, pairs)


def to_core(block):
    return send(block, lambda x, y, z, s: (x, y, z, 1 - s))


def along_y(block):
    return send(block, lambda x, y, z, s: (x, y + 1 - 2 * s, z, s))


def along_z(block):
    return send(block, lambda x, y, z, s: (x, y, z + 1 - 2 * s, s))


SLOTS = ((0, 3, 1, 2), (0, 1, 3, 2))


def swap(block, axis, turn):
    def move(x, y, z, s):
        apart = SLOTS[s][2 - turn]
        return (x ^ apart, y, z, s) if axis == "x" else (x, y ^ apart, z, s)

    return send(block, move)


def to_pair(block, far):
    return send(block, lambda x, y, z, s: (x, y, ((z + NZ - s) % NZ ^ far) + s, s))


def to_near(block):
    return to_pair(block, 1)


def after(value, *earlier):
    return lax.optimization_barrier((value, earlier))[0]


def split(value):
    high = value.astype(BF16)
    return high, (value - high.astype(F32)).astype(BF16)


def dot3(left, right, dims):
    lh, ll = split(left)
    rh, rl = split(right)
    d = (dims, ((), ()))
    out = lax.dot_general(lh, rh, d, preferred_element_type=F32)
    out += lax.dot_general(ll, rh, d, preferred_element_type=F32)
    return out + lax.dot_general(lh, rl, d, preferred_element_type=F32)


NN = ((1,), (0,))
TN = ((0,), (0,))


def fill_left(ref, row, place, value):
    deep = ref.shape[1] // 3
    high, low = split(value)
    m, k = value.shape
    ref[row : row + m, place : place + k] = high
    ref[row : row + m, deep + place : deep + place + k] = low
    ref[row : row + m, 2 * deep + place : 2 * deep + place + k] = high


def fill_right(ref, place, column, value):
    deep = ref.shape[0] // 3
    high, low = split(value)
    k, n = value.shape
    ref[place : place + k, column : column + n] = high
    ref[deep + place : deep + place + k, column : column + n] = high
    ref[2 * deep + place : 2 * deep + place + k, column : column + n] = low


def product(left, right):
    return jnp.dot(left, right, preferred_element_type=F32)


def exact(left, right):
    return jnp.dot(left, right, precision=lax.Precision.HIGHEST, preferred_element_type=F32)


def params(limit=16):
    return pltpu.CompilerParams(vmem_limit_bytes=limit * 1024 * 1024)


def cost(flops, moved):
    return pl.CostEstimate(flops=flops, bytes_accessed=moved, transcendentals=0)


VMEM = pl.BlockSpec(memory_space=pltpu.VMEM)
SMEM = pl.BlockSpec(memory_space=pltpu.SMEM)
HBM = pl.BlockSpec(memory_space=pltpu.HBM)
WIDE = 6 * B
SLAB = (NY, 2, Q, B)


def slab_product(at, step, own, other, even, odd, left, right, slabs, sems):
    y, s, slab = at[1], at[3], at[4 + step]
    copies = [
        pltpu.make_async_copy(ref.at[slab], slabs.at[n], sems.at[n]) for n, ref in enumerate((own, other))
    ]
    for copy in copies:
        copy.start()
    depth = even.shape[0] * Q
    for n, ref in enumerate((even, odd)):
        for panel in range(2):
            fill_right(right, n * depth, panel * B, ref[:, panel].reshape(depth, B))
    near = lax.rem(y + 3 + 2 * s, NY)
    for o in range(2):
        copies[o].wait()
        for n, first in enumerate((y, near)):
            blocks = [
                slabs[o, lax.rem(first + 2 * d, NY), core]
                for d in range(2)
                for core in (s, 1 - s)[: depth // 128]
            ]
            fill_left(left, o * B, n * depth, jnp.concatenate(blocks, axis=0).T)
    return product(left[...], right[...])


def slab_scratch(even):
    deep = 6 * even.shape[0] * Q
    return [
        pltpu.VMEM((2 * B, deep), BF16),
        pltpu.VMEM((deep, 2 * B), BF16),
        pltpu.VMEM((2,) + SLAB, F32),
        pltpu.SemaphoreType.DMA((2,)),
    ]


def multiply(place, step, sigma, other, even, odd, total=None):
    totals = [] if total is None else [total]

    def kernel(at, own_ref, other_ref, even_ref, odd_ref, *refs):
        s = at[3]
        out = refs[len(totals)]
        value = slab_product(at, step, own_ref, other_ref, even_ref, odd_ref, *refs[len(totals) + 1 :])
        for o, tile in enumerate((s, 1 - s)):
            part = value[o * B : (o + 1) * B]
            out[tile] = part if total is None else part + refs[0][tile]

    return pl.pallas_call(
        kernel,
        in_specs=[SMEM, HBM, HBM] + [VMEM] * (2 + len(totals)),
        out_specs=VMEM,
        out_shape=jax.ShapeDtypeStruct((2, B, 2 * B), F32),
        scratch_shapes=slab_scratch(even),
        input_output_aliases={5: 0} if totals else {},
        compiler_params=params(30),
        cost_estimate=cost(3 << 28, 2 << 20),
        name="multiply",
    )(place, sigma, other, even, odd, *totals)


N = 3 * B // 32


def along(y, core, sub):
    base = y if sub < 2 else y ^ SLOTS[core][2]
    other = base ^ SLOTS[core][1]
    return jnp.maximum(base, other) if sub % 2 else jnp.minimum(base, other)


def last_kernel(at, own, other, even, odd, total, weights, corner, pieces, whole, t_all, t_right, *scratch):
    x, y, s = at[2], at[1], at[3]
    value = slab_product(at, 4, own, other, even, odd, *scratch)
    for o, tile in enumerate((s, 1 - s)):
        t_all[tile] = total[tile] + value[o * B : (o + 1) * B]
    fill_right(t_right, 0, 0, t_all[...].reshape(2 * B, 2 * B))
    top = product(weights[:B], t_right[...])
    whole[:B] = top[:, :B]
    whole[B : 2 * B] = top[:, B:]
    whole[2 * B :] = product(weights[B:], t_right[:, B:])
    for core in range(2):
        for slot, apart in enumerate(SLOTS[core]):
            p = x ^ apart
            for sub in range(NY):
                start = (core * NX + p) * (NY * N) + along(y, core, sub) * N
                corner[core ^ s, slot, sub] = whole[pl.ds(pl.multiple_of(start, 8), N), :]
            rows = pl.ds(pl.multiple_of((p // 2 * 2 + core) * Q, 8), Q)
            pieces[core ^ s, slot] = t_all[lax.rem(p, 2), rows, :]


def last(place, sigma, other, even, odd, total, weights):
    return pl.pallas_call(
        last_kernel,
        in_specs=[SMEM, HBM, HBM] + [VMEM] * 4,
        out_specs=[VMEM, VMEM],
        out_shape=[
            jax.ShapeDtypeStruct((2, NX, NY, N, B), F32),
            jax.ShapeDtypeStruct((2, NX, Q, 2 * B), F32),
        ],
        scratch_shapes=[
            pltpu.VMEM((3 * B, B), F32),
            pltpu.VMEM((2, B, 2 * B), F32),
            pltpu.VMEM((WIDE, 2 * B), BF16),
        ]
        + slab_scratch(even),
        compiler_params=params(30),
        cost_estimate=cost(1 << 30, 2 << 20),
        name="last",
    )(place, sigma, other, even, odd, total, weights)


def invert_kernel(_, one_ref, zero_ref, out_one, out_zero, one, zero, sems):
    copies = [pltpu.make_async_copy(one_ref, one, sems.at[0]), pltpu.make_async_copy(zero_ref, zero, sems.at[1])]
    for copy in copies:
        copy.start()
    for copy in copies:
        copy.wait()
    row = lax.broadcasted_iota(jnp.int32, (HALF, HALF), 0)
    col = lax.broadcasted_iota(jnp.int32, (HALF, HALF), 1)
    blocks, inverses = [], []
    for ref in (one, zero):
        for k in range(2):
            block = ref[k * HALF : (k + 1) * HALF, k * HALF : (k + 1) * HALF]
            blocks.append(block)
            inverses.append(jnp.where(row == col, 1.0 / block, 0.0))
    below = jnp.logical_and(row == col + 1, row % 2 == 1)
    scales = [jnp.sum(i, axis=1, keepdims=True) for i in inverses]
    inverses = [
        i - r * jnp.where(below, b, 0.0) * jnp.sum(i, axis=0, keepdims=True)
        for b, i, r in zip(blocks, inverses, scales)
    ]
    size = 2
    while size < HALF:
        below = jnp.logical_and(
            row // (2 * size) == col // (2 * size),
            jnp.logical_and((row // size) % 2 == 1, (col // size) % 2 == 0),
        )
        middles = [exact(jnp.where(below, b, 0.0), i) for b, i in zip(blocks, inverses)]
        inverses = [i - exact(i, m) for i, m in zip(inverses, middles)]
        size *= 2
    for n, (ref, out) in enumerate(((one, out_one), (zero, out_zero))):
        top, bottom = inverses[2 * n], inverses[2 * n + 1]
        out[:HALF, :HALF] = top
        out[HALF:, HALF:] = bottom
        out[:HALF, HALF:] = jnp.zeros((HALF, HALF), F32)
        out[HALF:, :HALF] = -exact(bottom, exact(ref[HALF:, :HALF], top))


def invert(place, one, zero):
    tile = jax.ShapeDtypeStruct((B, B), F32)
    return pl.pallas_call(
        invert_kernel,
        in_specs=[SMEM, HBM, HBM],
        out_specs=[VMEM, VMEM],
        out_shape=[tile, tile],
        scratch_shapes=[pltpu.VMEM((B, B), F32), pltpu.VMEM((B, B), F32), pltpu.SemaphoreType.DMA((2,))],
        compiler_params=params(),
        cost_estimate=cost(1 << 32, 1 << 20),
        name="invert",
    )(place, one, zero)


def constants_kernel(x1_ref, x0_ref, link, z_terms, zt_terms, base):
    x1, x0 = x1_ref[...], x0_ref[...]
    hl = dot3(link[...], x0, NN)
    top = -dot3(x1, hl, NN)
    none = jnp.zeros((B, B), F32)
    for row, column, block in ((0, 0, x1), (0, B, top), (B, 0, none), (B, B, x0)):
        fill_right(z_terms, row, column, block)
        fill_left(zt_terms, column, row, block.T)
    inv1 = dot3(x1, x1, TN)
    cross = dot3(inv1, hl, NN)
    base[:B] = inv1
    base[B : 2 * B] = -cross
    base[2 * B :] = dot3(x0, x0, TN) + dot3(hl, cross, TN)


def constants(x1, x0, link):
    return pl.pallas_call(
        constants_kernel,
        in_specs=[VMEM] * 3,
        out_specs=[VMEM] * 3,
        out_shape=[
            jax.ShapeDtypeStruct((WIDE, 2 * B), BF16),
            jax.ShapeDtypeStruct((2 * B, WIDE), BF16),
            jax.ShapeDtypeStruct((3 * B, B), F32),
        ],
        compiler_params=params(),
        cost_estimate=cost(1 << 29, 3 << 20),
        name="constants",
    )(x1, x0, link)


def weigh_kernel(at, mine, others, weights, rows):
    x, y, s = at[2], at[1], at[3]
    for tile in range(2):
        for g in range(2):
            for core in range(2):
                near = (tile ^ lax.rem(x, 2)) * 2 + (g ^ lax.rem(y, 2))
                start = ((tile * 2 + g) * 2 + core) * Q
                for panel in range(2):
                    block = jnp.where(s == core, mine[near, panel], others[near, panel])
                    rows[start : start + Q, panel * B : (panel + 1) * B] = block
    fill_left(weights, 0, 0, rows[...].T)


def weigh(place, mine, others):
    return pl.pallas_call(
        weigh_kernel,
        in_specs=[SMEM] + [VMEM] * 2,
        out_specs=VMEM,
        out_shape=jax.ShapeDtypeStruct((2 * B, WIDE), BF16),
        scratch_shapes=[pltpu.VMEM((2 * B, 2 * B), F32)],
        compiler_params=params(),
        cost_estimate=cost(1 << 28, 3 << 20),
        name="weigh",
    )(place, mine, others)


def rows_kernel(a, b, z_terms, sigmas, left):
    fill_left(left, 0, 0, a[...] + b[...])
    both = product(left[...], z_terms[...])
    sigmas[0] = -both[:, :B]
    sigmas[1] = -both[:, B:]


def rows(a, b, z_terms):
    return pl.pallas_call(
        rows_kernel,
        in_specs=[VMEM] * 3,
        out_specs=VMEM,
        out_shape=jax.ShapeDtypeStruct((2, Q, B), F32),
        scratch_shapes=[pltpu.VMEM((Q, WIDE), BF16)],
        compiler_params=params(),
        cost_estimate=cost(1 << 27, 2 << 20),
        name="rows",
    )(a, b, z_terms)


def finish_kernel(at, mine, other, z_terms, zt_terms, base, s11, s10, s00, whole, left, right):
    x, y, s = at[2], at[1], at[3]
    for core in range(2):

        def place_all(ref):
            for slot, apart in enumerate(SLOTS[core]):
                for sub in range(NY):
                    start = (core * NX + (x ^ apart)) * (NY * N) + along(y, core, sub) * N
                    whole[pl.ds(pl.multiple_of(start, 8), N), :] = ref[slot, sub // 2, sub % 2]

        @pl.when(s == core)
        def _():
            place_all(mine)

        @pl.when(s != core)
        def _():
            place_all(other)

    crossed = whole[B : 2 * B]
    fill_left(left, 0, 0, whole[:B])
    fill_left(left, 0, B, crossed)
    fill_left(left, B, 0, crossed.T)
    fill_left(left, B, B, whole[2 * B :])
    fill_right(right, 0, 0, product(left[...], z_terms[...]))
    top = product(zt_terms[:B], right[...])
    s11[...] = top[:, :B] + base[:B]
    s10[...] = top[:, B:] + base[B : 2 * B]
    s00[...] = product(zt_terms[B:], right[:, B:]) + base[2 * B :]


def finish(place, mine, other, z_terms, zt_terms, base):
    tile = jax.ShapeDtypeStruct((B, B), F32)
    return pl.pallas_call(
        finish_kernel,
        in_specs=[SMEM] + [VMEM] * 5,
        out_specs=[VMEM] * 3,
        out_shape=[tile, tile, tile],
        scratch_shapes=[
            pltpu.VMEM((3 * B, B), F32),
            pltpu.VMEM((2 * B, WIDE), BF16),
            pltpu.VMEM((WIDE, 2 * B), BF16),
        ],
        compiler_params=params(),
        cost_estimate=cost(1 << 28, 3 << 20),
        name="finish",
    )(place, mine, other, z_terms, zt_terms, base)


def body(sigma, p1, p0, link, diag_one, diag_zero):
    x, y, z, s = (lax.axis_index(name).astype(jnp.int32) for name in ("x", "y", "z", "s"))
    way = 2 * s - 1
    place = jnp.stack([z, y, x, s] + [lax.rem(z + NZ + j * way, NZ) for j in range(5)])

    view = (NZ,) + SLAB
    own = jnp.stack([p1, p0])[None]
    a = jnp.concatenate([own, to_core(own)], axis=0)
    y2 = send(own, lambda x, y, z, s: (x, y + 2, z, s))
    a1 = along_z(a)
    b = jnp.concatenate([after(y2, a), to_core(y2)], axis=0)
    b1 = along_z(b)
    a2 = along_z(after(a1, b))

    sigma_other = to_core(after(sigma, b, a1)).reshape(view)
    sigma = sigma.reshape(view)
    even = jnp.concatenate([own, after(y2, a1)], axis=0)
    odd = along_y(even)
    b1, odd = after((b1, odd), b1, odd)
    b2 = along_z(b1)
    z1 = jnp.concatenate([a1, b1], axis=0)
    e1 = along_y(z1)
    pair = jnp.concatenate([own, jnp.where(y % 2 == s, odd[1:], odd[:1])], axis=0)
    a3 = along_z(after(a2, b1))
    crossed = send(after(pair, a2), lambda x, y, z, s: (x ^ 2, y, z, s))
    total = multiply(place, 0, sigma, sigma_other, even, odd)

    b2 = after(b2, a2)
    b3 = along_z(b2)
    z2 = jnp.concatenate([a2, b2], axis=0)
    e2 = along_y(z2)
    a3 = after(a3, b2)
    first = jnp.where(x // 2 == y % 2, pair, after(crossed, b2))
    second = send(first, lambda x, y, z, s: (x ^ 1, y, z, s))

    b3 = after(b3, a3, total)
    z4 = along_z(jnp.concatenate([a3[:1], b3[:1]], axis=0))
    z3 = jnp.concatenate([a3, b3], axis=0)
    e3 = along_y(z3)
    mine = jnp.concatenate([first, after(second, b3)], axis=0)
    others = to_core(mine)
    total = multiply(place, 1, sigma, sigma_other, z1, e1, total)

    z4, others, e2 = after((z4, others, e2), z4, others, total, e2)
    e4 = along_y(z4)
    total = multiply(place, 2, sigma, sigma_other, z2, e2, total)
    weights = weigh(place, mine, others)
    total = multiply(place, 3, sigma, sigma_other, z3, e3, total)
    corner, pieces = last(place, sigma, sigma_other, z4, e4, total, weights)

    part = corner[0] + to_core(corner[1])
    came = swap(part[2:], "x", 0)
    q = pieces[0] + to_core(pieces[1])
    x1, x0 = invert(after(place, part), diag_one, diag_zero)
    part = part[:2] + after(came, x1, x0, q)
    came = swap(part[1], "x", 1)
    z_terms, zt_terms, base = constants(x1, x0, after(link, part))
    part = part[0] + after(came, base)
    q = q[:2] + swap(q[2:], "x", 0)
    part = part[:2] + swap(part[2:], "y", 0)
    part = part + swap(part, "y", 1)
    part = after(part, q)
    part = part + to_near(part)
    came = swap(q[1], "x", 1)
    a, b, c = (to_pair(part, far) for far in (2, 4, 6))
    part = after((part + a) + (b + c), came)
    sigmas = rows(q[0], came, z_terms)
    part = jnp.stack([part, after(swap(part, "y", 0), sigmas)])
    sigmas = send(sigmas, lambda x, y, z, s: (y % 2 * 2 + x % 2, y // 2 * 2 + x // 2, z, s))
    part = jnp.stack([part, swap(part, "x", 1)])
    mine = after(jnp.concatenate([part, swap(part, "x", 0)], axis=0), sigmas)
    s11, s10, s00 = finish(place, mine, to_core(mine), z_terms, zt_terms, base)
    return sigmas[0], s11, sigmas[1], s10, s00


def solution(mesh):
    mesh = Mesh(mesh.devices.reshape(NX, NZ, NY, 2), AXES)
    in_specs = (P("x", AXES[1:]), P(AXES, None), P(AXES, None), P(), P(), P())
    out_specs = (P(AXES, None), P(), P(AXES, None), P(), P())
    return jax.shard_map(body, mesh=mesh, in_specs=in_specs, out_specs=out_specs, check_vma=False)
```

```python
import jax
import jax.numpy as jnp
from jax import lax
from jax.experimental import pallas as pl
from jax.experimental.pallas import tpu as pltpu
from jax.sharding import Mesh, PartitionSpec as P

F32 = jnp.float32
BF16 = jnp.bfloat16
AXES = ("x", "z", "y", "s")
NX, NY, NZ = 4, 4, 8
B = 256
Q = 64
HALF = 128


def device(x, y, z, s):
    return (x % NX) * 64 + (z % NZ) * 8 + (y % NY) * 2 + s


def send(block, move):
    pairs = [
        (device(x, y, z, s), device(*move(x, y, z, s)))
        for x in range(NX)
        for z in range(NZ)
        for y in range(NY)
        for s in range(2)
    ]
    return lax.ppermute(block, AXES, pairs)


def to_core(block):
    return send(block, lambda x, y, z, s: (x, y, z, 1 - s))


def along_y(block):
    return send(block, lambda x, y, z, s: (x, y + 1 - 2 * s, z, s))


def along_z(block):
    return send(block, lambda x, y, z, s: (x, y, z + 1 - 2 * s, s))


SLOTS = ((0, 3, 1, 2), (0, 1, 3, 2))


def swap(block, axis, turn):
    def move(x, y, z, s):
        apart = SLOTS[s][2 - turn]
        return (x ^ apart, y, z, s) if axis == "x" else (x, y ^ apart, z, s)

    return send(block, move)


def to_pair(block, far):
    return send(block, lambda x, y, z, s: (x, y, ((z + NZ - s) % NZ ^ far) + s, s))


def to_near(block):
    return to_pair(block, 1)


def after(value, *earlier):
    return lax.optimization_barrier((value, earlier))[0]


def split(value):
    high = value.astype(BF16)
    return high, (value - high.astype(F32)).astype(BF16)


def dot3(left, right, dims):
    lh, ll = split(left)
    rh, rl = split(right)
    d = (dims, ((), ()))
    out = lax.dot_general(lh, rh, d, preferred_element_type=F32)
    out += lax.dot_general(ll, rh, d, preferred_element_type=F32)
    return out + lax.dot_general(lh, rl, d, preferred_element_type=F32)


NN = ((1,), (0,))
TN = ((0,), (0,))


def fill_left(ref, row, place, value):
    deep = ref.shape[1] // 3
    high, low = split(value)
    m, k = value.shape
    ref[row : row + m, place : place + k] = high
    ref[row : row + m, deep + place : deep + place + k] = low
    ref[row : row + m, 2 * deep + place : 2 * deep + place + k] = high


def fill_right(ref, place, column, value):
    deep = ref.shape[0] // 3
    high, low = split(value)
    k, n = value.shape
    ref[place : place + k, column : column + n] = high
    ref[deep + place : deep + place + k, column : column + n] = high
    ref[2 * deep + place : 2 * deep + place + k, column : column + n] = low


def product(left, right):
    return jnp.dot(left, right, preferred_element_type=F32)


def exact(left, right):
    return jnp.dot(left, right, precision=lax.Precision.HIGHEST, preferred_element_type=F32)


def params(limit=16):
    return pltpu.CompilerParams(vmem_limit_bytes=limit * 1024 * 1024)


def cost(flops, moved):
    return pl.CostEstimate(flops=flops, bytes_accessed=moved, transcendentals=0)


VMEM = pl.BlockSpec(memory_space=pltpu.VMEM)
SMEM = pl.BlockSpec(memory_space=pltpu.SMEM)
HBM = pl.BlockSpec(memory_space=pltpu.HBM)
WIDE = 6 * B
SLAB = (NY, 2, Q, B)


def stage(place, sigma):
    def kernel(at, ref, out, sems):
        copies = [pltpu.make_async_copy(ref.at[at[4 + n]], out.at[n], sems.at[n]) for n in range(5)]
        for copy in copies:
            copy.start()
        for copy in copies:
            copy.wait()

    return pl.pallas_call(
        kernel,
        in_specs=[SMEM, HBM],
        out_specs=VMEM,
        out_shape=jax.ShapeDtypeStruct((5,) + SLAB, F32),
        scratch_shapes=[pltpu.SemaphoreType.DMA((5,))],
        compiler_params=params(),
        cost_estimate=cost(0, 5 << 20),
        name="stage",
    )(place, sigma)


def slab_product(at, step, own, other, even, odd, left, right, slabs, sems):
    y, s, slab = at[1], at[3], at[4 + step]
    copy = pltpu.make_async_copy(other.at[slab], slabs, sems.at[0])
    copy.start()
    depth = even.shape[0] * Q
    for n, ref in enumerate((even, odd)):
        for panel in range(2):
            fill_right(right, n * depth, panel * B, ref[:, panel].reshape(depth, B))
    near = lax.rem(y + 3 + 2 * s, NY)
    for o in range(2):
        if o == 1:
            copy.wait()
        for n, first in enumerate((y, near)):
            blocks = [
                (slabs if o else own.at[step])[lax.rem(first + 2 * d, NY), core]
                for d in range(2)
                for core in (s, 1 - s)[: depth // 128]
            ]
            fill_left(left, o * B, n * depth, jnp.concatenate(blocks, axis=0).T)
    return product(left[...], right[...])


def slab_scratch(even):
    deep = 6 * even.shape[0] * Q
    return [
        pltpu.VMEM((2 * B, deep), BF16),
        pltpu.VMEM((deep, 2 * B), BF16),
        pltpu.VMEM(SLAB, F32),
        pltpu.SemaphoreType.DMA((1,)),
    ]


def multiply(place, step, sigma, other, even, odd, total=None):
    totals = [] if total is None else [total]

    def kernel(at, own_ref, other_ref, even_ref, odd_ref, *refs):
        s = at[3]
        out = refs[len(totals)]
        value = slab_product(at, step, own_ref, other_ref, even_ref, odd_ref, *refs[len(totals) + 1 :])
        for o, tile in enumerate((s, 1 - s)):
            part = value[o * B : (o + 1) * B]
            out[tile] = part if total is None else part + refs[0][tile]

    return pl.pallas_call(
        kernel,
        in_specs=[SMEM, VMEM, HBM] + [VMEM] * (2 + len(totals)),
        out_specs=VMEM,
        out_shape=jax.ShapeDtypeStruct((2, B, 2 * B), F32),
        scratch_shapes=slab_scratch(even),
        input_output_aliases={5: 0} if totals else {},
        compiler_params=params(30),
        cost_estimate=cost(3 << 28, 2 << 20),
        name="multiply",
    )(place, sigma, other, even, odd, *totals)


N = 3 * B // 32


def along(y, core, sub):
    base = y if sub < 2 else y ^ SLOTS[core][2]
    other = base ^ SLOTS[core][1]
    return jnp.maximum(base, other) if sub % 2 else jnp.minimum(base, other)


def last_kernel(at, own, other, even, odd, total, weights, corner, pieces, whole, t_all, t_right, *scratch):
    x, y, s = at[2], at[1], at[3]
    value = slab_product(at, 4, own, other, even, odd, *scratch)
    for o, tile in enumerate((s, 1 - s)):
        t_all[tile] = total[tile] + value[o * B : (o + 1) * B]
    fill_right(t_right, 0, 0, t_all[...].reshape(2 * B, 2 * B))
    top = product(weights[:B], t_right[...])
    whole[:B] = top[:, :B]
    whole[B : 2 * B] = top[:, B:]
    whole[2 * B :] = product(weights[B:], t_right[:, B:])
    for core in range(2):
        for slot, apart in enumerate(SLOTS[core]):
            p = x ^ apart
            for sub in range(NY):
                start = (core * NX + p) * (NY * N) + along(y, core, sub) * N
                corner[core ^ s, slot, sub] = whole[pl.ds(pl.multiple_of(start, 8), N), :]
            rows = pl.ds(pl.multiple_of((p // 2 * 2 + core) * Q, 8), Q)
            pieces[core ^ s, slot] = t_all[lax.rem(p, 2), rows, :]


def last(place, sigma, other, even, odd, total, weights):
    return pl.pallas_call(
        last_kernel,
        in_specs=[SMEM, VMEM, HBM] + [VMEM] * 4,
        out_specs=[VMEM, VMEM],
        out_shape=[
            jax.ShapeDtypeStruct((2, NX, NY, N, B), F32),
            jax.ShapeDtypeStruct((2, NX, Q, 2 * B), F32),
        ],
        scratch_shapes=[
            pltpu.VMEM((3 * B, B), F32),
            pltpu.VMEM((2, B, 2 * B), F32),
            pltpu.VMEM((WIDE, 2 * B), BF16),
        ]
        + slab_scratch(even),
        compiler_params=params(30),
        cost_estimate=cost(1 << 30, 2 << 20),
        name="last",
    )(place, sigma, other, even, odd, total, weights)


def invert_kernel(_, one_ref, zero_ref, out_one, out_zero, one, zero, sems):
    copies = [pltpu.make_async_copy(one_ref, one, sems.at[0]), pltpu.make_async_copy(zero_ref, zero, sems.at[1])]
    for copy in copies:
        copy.start()
    for copy in copies:
        copy.wait()
    row = lax.broadcasted_iota(jnp.int32, (HALF, HALF), 0)
    col = lax.broadcasted_iota(jnp.int32, (HALF, HALF), 1)
    blocks, inverses = [], []
    for ref in (one, zero):
        for k in range(2):
            block = ref[k * HALF : (k + 1) * HALF, k * HALF : (k + 1) * HALF]
            blocks.append(block)
            inverses.append(jnp.where(row == col, 1.0 / block, 0.0))
    below = jnp.logical_and(row == col + 1, row % 2 == 1)
    scales = [jnp.sum(i, axis=1, keepdims=True) for i in inverses]
    inverses = [
        i - r * jnp.where(below, b, 0.0) * jnp.sum(i, axis=0, keepdims=True)
        for b, i, r in zip(blocks, inverses, scales)
    ]
    size = 2
    while size < HALF:
        below = jnp.logical_and(
            row // (2 * size) == col // (2 * size),
            jnp.logical_and((row // size) % 2 == 1, (col // size) % 2 == 0),
        )
        middles = [exact(jnp.where(below, b, 0.0), i) for b, i in zip(blocks, inverses)]
        inverses = [i - exact(i, m) for i, m in zip(inverses, middles)]
        size *= 2
    for n, (ref, out) in enumerate(((one, out_one), (zero, out_zero))):
        top, bottom = inverses[2 * n], inverses[2 * n + 1]
        out[:HALF, :HALF] = top
        out[HALF:, HALF:] = bottom
        out[:HALF, HALF:] = jnp.zeros((HALF, HALF), F32)
        out[HALF:, :HALF] = -exact(bottom, exact(ref[HALF:, :HALF], top))


def invert(place, one, zero):
    tile = jax.ShapeDtypeStruct((B, B), F32)
    return pl.pallas_call(
        invert_kernel,
        in_specs=[SMEM, HBM, HBM],
        out_specs=[VMEM, VMEM],
        out_shape=[tile, tile],
        scratch_shapes=[pltpu.VMEM((B, B), F32), pltpu.VMEM((B, B), F32), pltpu.SemaphoreType.DMA((2,))],
        compiler_params=params(),
        cost_estimate=cost(1 << 32, 1 << 20),
        name="invert",
    )(place, one, zero)


def constants_kernel(x1_ref, x0_ref, link, z_terms, zt_terms, base):
    x1, x0 = x1_ref[...], x0_ref[...]
    hl = dot3(link[...], x0, NN)
    top = -dot3(x1, hl, NN)
    none = jnp.zeros((B, B), F32)
    for row, column, block in ((0, 0, x1), (0, B, top), (B, 0, none), (B, B, x0)):
        fill_right(z_terms, row, column, block)
        fill_left(zt_terms, column, row, block.T)
    inv1 = dot3(x1, x1, TN)
    cross = dot3(inv1, hl, NN)
    base[:B] = inv1
    base[B : 2 * B] = -cross
    base[2 * B :] = dot3(x0, x0, TN) + dot3(hl, cross, TN)


def constants(x1, x0, link):
    return pl.pallas_call(
        constants_kernel,
        in_specs=[VMEM] * 3,
        out_specs=[VMEM] * 3,
        out_shape=[
            jax.ShapeDtypeStruct((WIDE, 2 * B), BF16),
            jax.ShapeDtypeStruct((2 * B, WIDE), BF16),
            jax.ShapeDtypeStruct((3 * B, B), F32),
        ],
        compiler_params=params(),
        cost_estimate=cost(1 << 29, 3 << 20),
        name="constants",
    )(x1, x0, link)


def weigh_kernel(at, mine, others, weights, rows):
    x, y, s = at[2], at[1], at[3]
    for tile in range(2):
        for g in range(2):
            for core in range(2):
                near = (tile ^ lax.rem(x, 2)) * 2 + (g ^ lax.rem(y, 2))
                start = ((tile * 2 + g) * 2 + core) * Q
                for panel in range(2):
                    block = jnp.where(s == core, mine[near, panel], others[near, panel])
                    rows[start : start + Q, panel * B : (panel + 1) * B] = block
    fill_left(weights, 0, 0, rows[...].T)


def weigh(place, mine, others):
    return pl.pallas_call(
        weigh_kernel,
        in_specs=[SMEM] + [VMEM] * 2,
        out_specs=VMEM,
        out_shape=jax.ShapeDtypeStruct((2 * B, WIDE), BF16),
        scratch_shapes=[pltpu.VMEM((2 * B, 2 * B), F32)],
        compiler_params=params(),
        cost_estimate=cost(1 << 28, 3 << 20),
        name="weigh",
    )(place, mine, others)


def rows_kernel(a, b, z_terms, s1, s0, left):
    fill_left(left, 0, 0, a[...] + b[...])
    both = product(left[...], z_terms[...])
    s1[...] = -both[:, :B]
    s0[...] = -both[:, B:]


def rows(a, b, z_terms):
    out = jax.ShapeDtypeStruct((Q, B), F32)
    return pl.pallas_call(
        rows_kernel,
        in_specs=[VMEM] * 3,
        out_specs=[VMEM] * 2,
        out_shape=[out, out],
        scratch_shapes=[pltpu.VMEM((Q, WIDE), BF16)],
        compiler_params=params(),
        cost_estimate=cost(1 << 27, 2 << 20),
        name="rows",
    )(a, b, z_terms)


def finish_kernel(at, mine, other, z_terms, zt_terms, base, s11, s10, s00, whole, left, right):
    x, y, s = at[2], at[1], at[3]
    for core in range(2):

        def place_all(ref):
            for slot, apart in enumerate(SLOTS[core]):
                for sub in range(NY):
                    start = (core * NX + (x ^ apart)) * (NY * N) + along(y, core, sub) * N
                    whole[pl.ds(pl.multiple_of(start, 8), N), :] = ref[slot, sub // 2, sub % 2]

        @pl.when(s == core)
        def _():
            place_all(mine)

        @pl.when(s != core)
        def _():
            place_all(other)

    crossed = whole[B : 2 * B]
    fill_left(left, 0, 0, whole[:B])
    fill_left(left, 0, B, crossed)
    fill_left(left, B, 0, crossed.T)
    fill_left(left, B, B, whole[2 * B :])
    fill_right(right, 0, 0, product(left[...], z_terms[...]))
    top = product(zt_terms[:B], right[...])
    s11[...] = top[:, :B] + base[:B]
    s10[...] = top[:, B:] + base[B : 2 * B]
    s00[...] = product(zt_terms[B:], right[:, B:]) + base[2 * B :]


def finish(place, mine, other, z_terms, zt_terms, base):
    tile = jax.ShapeDtypeStruct((B, B), F32)
    return pl.pallas_call(
        finish_kernel,
        in_specs=[SMEM] + [VMEM] * 5,
        out_specs=[VMEM] * 3,
        out_shape=[tile, tile, tile],
        scratch_shapes=[
            pltpu.VMEM((3 * B, B), F32),
            pltpu.VMEM((2 * B, WIDE), BF16),
            pltpu.VMEM((WIDE, 2 * B), BF16),
        ],
        compiler_params=params(),
        cost_estimate=cost(1 << 28, 3 << 20),
        name="finish",
    )(place, mine, other, z_terms, zt_terms, base)


def body(sigma, p1, p0, link, diag_one, diag_zero):
    x, y, z, s = (lax.axis_index(name).astype(jnp.int32) for name in ("x", "y", "z", "s"))
    way = 2 * s - 1
    place = jnp.stack([z, y, x, s] + [lax.rem(z + NZ + j * way, NZ) for j in range(5)])

    view = (NZ,) + SLAB
    own = jnp.stack([p1, p0])[None]
    a = jnp.concatenate([own, to_core(own)], axis=0)
    y2 = send(own, lambda x, y, z, s: (x, y + 2, z, s))
    a1 = along_z(a)
    staged = stage(after(place, a), sigma.reshape(view))
    y2 = after(y2, a, staged)
    b = jnp.concatenate([y2, to_core(y2)], axis=0)
    b1 = along_z(b)
    a2 = along_z(after(a1, b))

    sigma_other = to_core(after(sigma, b, a1)).reshape(view)
    even = jnp.concatenate([own, after(y2, a1)], axis=0)
    odd = along_y(even)
    b1, odd = after((b1, odd), b1, odd)
    b2 = along_z(b1)
    z1 = jnp.concatenate([a1, b1], axis=0)
    e1 = along_y(z1)
    pair = jnp.concatenate([own, jnp.where(y % 2 == s, odd[1:], odd[:1])], axis=0)
    a3 = along_z(after(a2, b1))
    crossed = send(after(pair, a2), lambda x, y, z, s: (x ^ 2, y, z, s))

    b2 = after(b2, a2)
    b3 = along_z(b2)
    z2 = jnp.concatenate([a2, b2], axis=0)
    e2 = along_y(z2)
    a3 = after(a3, b2)
    total = multiply(place, 0, staged, sigma_other, even, odd)

    b3, crossed = after((b3, crossed), b3, crossed, a3, total)
    z4 = along_z(jnp.concatenate([a3[:1], b3[:1]], axis=0))
    z3 = jnp.concatenate([a3, b3], axis=0)
    e3 = along_y(z3)
    first = jnp.where(x // 2 == y % 2, pair, crossed)
    second = send(first, lambda x, y, z, s: (x ^ 1, y, z, s))
    total = multiply(place, 1, staged, sigma_other, z1, e1, total)

    z4, second, e2 = after((z4, second, e2), z4, second, e2, total)
    e4 = along_y(z4)
    mine = jnp.concatenate([first, second], axis=0)
    others = to_core(mine)
    total = multiply(place, 2, staged, sigma_other, z2, e2, total)
    weights = weigh(place, mine, others)
    total = multiply(place, 3, staged, sigma_other, z3, e3, total)
    corner, pieces = last(place, staged, sigma_other, z4, e4, total, weights)

    part = corner[0] + to_core(corner[1])
    came = swap(part[2:], "x", 0)
    q = pieces[0] + to_core(pieces[1])
    x1, x0 = invert(after(place, part), diag_one, diag_zero)
    part = part[:2] + after(came, x1, x0, q)
    came = swap(part[1], "x", 1)
    z_terms, zt_terms, base = constants(x1, x0, after(link, part))
    part = part[0] + after(came, base)
    q = q[:2] + swap(q[2:], "x", 0)
    part = part[:2] + swap(part[2:], "y", 0)
    part = part + swap(part, "y", 1)
    part = after(part, q)
    part = part + to_near(part)
    came = swap(q[1], "x", 1)
    a, b, c = (to_pair(part, far) for far in (2, 4, 6))
    part = after((part + a) + (b + c), came)
    s1, s0 = rows(q[0], came, z_terms)
    part = jnp.stack([part, after(swap(part, "y", 0), s1, s0)])

    def home(block):
        return send(block, lambda x, y, z, s: (y % 2 * 2 + x % 2, y // 2 * 2 + x // 2, z, s))

    sigmas = home(jnp.stack([s1, s0]))
    part = jnp.stack([part, swap(part, "x", 1)])
    mine = jnp.concatenate([part, swap(part, "x", 0)], axis=0)
    s11, s10, s00 = finish(place, mine, to_core(mine), z_terms, zt_terms, base)
    sigmas = after(sigmas, s11)
    s1, s0 = sigmas[0], sigmas[1]
    return s1, s11, s0, s10, s00


def solution(mesh):
    mesh = Mesh(mesh.devices.reshape(NX, NZ, NY, 2), AXES)
    in_specs = (P("x", AXES[1:]), P(AXES, None), P(AXES, None), P(), P(), P())
    out_specs = (P(AXES, None), P(), P(AXES, None), P(), P())
    return jax.shard_map(body, mesh=mesh, in_specs=in_specs, out_specs=out_specs, check_vma=False)
```

```python
import jax
import jax.numpy as jnp
from jax import lax
from jax.experimental import pallas as pl
from jax.experimental.pallas import tpu as pltpu
from jax.sharding import Mesh, PartitionSpec as P

F32 = jnp.float32
BF16 = jnp.bfloat16
AXES = ("x", "z", "y", "s")
NX, NY, NZ = 4, 4, 8
B = 256
Q = 64
HALF = 128


def device(x, y, z, s):
    return (x % NX) * 64 + (z % NZ) * 8 + (y % NY) * 2 + s


def send(block, move):
    pairs = [
        (device(x, y, z, s), device(*move(x, y, z, s)))
        for x in range(NX)
        for z in range(NZ)
        for y in range(NY)
        for s in range(2)
    ]
    return lax.ppermute(block, AXES, pairs)


def to_core(block):
    return send(block, lambda x, y, z, s: (x, y, z, 1 - s))


def along_y(block):
    return send(block, lambda x, y, z, s: (x, y + 1 - 2 * s, z, s))


def along_z(block):
    return send(block, lambda x, y, z, s: (x, y, z + 1 - 2 * s, s))


SLOTS = ((0, 3, 1, 2), (0, 1, 3, 2))


def swap(block, axis, turn):
    def move(x, y, z, s):
        apart = SLOTS[s][2 - turn]
        return (x ^ apart, y, z, s) if axis == "x" else (x, y ^ apart, z, s)

    return send(block, move)


def to_pair(block, far):
    return send(block, lambda x, y, z, s: (x, y, ((z + NZ - s) % NZ ^ far) + s, s))


def to_pair_y(block):
    return send(block, lambda x, y, z, s: (x, y ^ SLOTS[s][1], ((z + NZ - s) % NZ ^ 1) + s, s))


def to_second_x(block):
    return swap(block, "x", 1)


def to_first_y(block):
    return swap(block, "y", 0)


def to_both(block):
    return send(block, lambda x, y, z, s: (x ^ SLOTS[s][1], y ^ SLOTS[s][2], z, s))


def after(value, *earlier):
    return lax.optimization_barrier((value, earlier))[0]


def split(value):
    high = value.astype(BF16)
    return high, (value - high.astype(F32)).astype(BF16)


def dot3(left, right, dims):
    lh, ll = split(left)
    rh, rl = split(right)
    d = (dims, ((), ()))
    out = lax.dot_general(lh, rh, d, preferred_element_type=F32)
    out += lax.dot_general(ll, rh, d, preferred_element_type=F32)
    return out + lax.dot_general(lh, rl, d, preferred_element_type=F32)


NN = ((1,), (0,))
TN = ((0,), (0,))


def fill_left(ref, row, place, value):
    deep = ref.shape[1] // 3
    high, low = split(value)
    m, k = value.shape
    ref[row : row + m, place : place + k] = high
    ref[row : row + m, deep + place : deep + place + k] = low
    ref[row : row + m, 2 * deep + place : 2 * deep + place + k] = high


def fill_right(ref, place, column, value):
    deep = ref.shape[0] // 3
    high, low = split(value)
    k, n = value.shape
    ref[place : place + k, column : column + n] = high
    ref[deep + place : deep + place + k, column : column + n] = high
    ref[2 * deep + place : 2 * deep + place + k, column : column + n] = low


def product(left, right):
    return jnp.dot(left, right, preferred_element_type=F32)


def exact(left, right):
    return jnp.dot(left, right, precision=lax.Precision.HIGHEST, preferred_element_type=F32)


def params(limit=16):
    return pltpu.CompilerParams(vmem_limit_bytes=limit * 1024 * 1024)


def cost(flops, moved):
    return pl.CostEstimate(flops=flops, bytes_accessed=moved, transcendentals=0)


VMEM = pl.BlockSpec(memory_space=pltpu.VMEM)
SMEM = pl.BlockSpec(memory_space=pltpu.SMEM)
HBM = pl.BlockSpec(memory_space=pltpu.HBM)
WIDE = 6 * B
SLAB = (NY, 2, Q, B)


def stage(place, sigma):
    def kernel(at, ref, out, sems):
        copies = [pltpu.make_async_copy(ref.at[at[4 + n]], out.at[n], sems.at[n]) for n in range(5)]
        for copy in copies:
            copy.start()
        for copy in copies:
            copy.wait()

    return pl.pallas_call(
        kernel,
        in_specs=[SMEM, HBM],
        out_specs=VMEM,
        out_shape=jax.ShapeDtypeStruct((5,) + SLAB, F32),
        scratch_shapes=[pltpu.SemaphoreType.DMA((5,))],
        compiler_params=params(),
        cost_estimate=cost(0, 5 << 20),
        name="stage",
    )(place, sigma)


def slab_product(at, step, own, other, even, odd, left, right, slabs, sems):
    y, s, slab = at[1], at[3], at[4 + step]
    copy = pltpu.make_async_copy(other.at[slab], slabs, sems.at[0])
    copy.start()
    depth = even.shape[0] * Q
    for n, ref in enumerate((even, odd)):
        for panel in range(2):
            fill_right(right, n * depth, panel * B, ref[:, panel].reshape(depth, B))
    near = lax.rem(y + 3 + 2 * s, NY)
    for o in range(2):
        if o == 1:
            copy.wait()
        for n, first in enumerate((y, near)):
            blocks = [
                (slabs if o else own.at[step])[lax.rem(first + 2 * d, NY), core]
                for d in range(2)
                for core in (s, 1 - s)[: depth // 128]
            ]
            fill_left(left, o * B, n * depth, jnp.concatenate(blocks, axis=0).T)
    return product(left[...], right[...])


def slab_scratch(even):
    deep = 6 * even.shape[0] * Q
    return [
        pltpu.VMEM((2 * B, deep), BF16),
        pltpu.VMEM((deep, 2 * B), BF16),
        pltpu.VMEM(SLAB, F32),
        pltpu.SemaphoreType.DMA((1,)),
    ]


def multiply(place, step, sigma, other, even, odd, total=None):
    totals = [] if total is None else [total]

    def kernel(at, own_ref, other_ref, even_ref, odd_ref, *refs):
        s = at[3]
        out = refs[len(totals)]
        value = slab_product(at, step, own_ref, other_ref, even_ref, odd_ref, *refs[len(totals) + 1 :])
        for o, tile in enumerate((s, 1 - s)):
            part = value[o * B : (o + 1) * B]
            out[tile] = part if total is None else part + refs[0][tile]

    return pl.pallas_call(
        kernel,
        in_specs=[SMEM, VMEM, HBM] + [VMEM] * (2 + len(totals)),
        out_specs=VMEM,
        out_shape=jax.ShapeDtypeStruct((2, B, 2 * B), F32),
        scratch_shapes=slab_scratch(even),
        input_output_aliases={5: 0} if totals else {},
        compiler_params=params(30),
        cost_estimate=cost(3 << 28, 2 << 20),
        name="multiply",
    )(place, sigma, other, even, odd, *totals)


N = 3 * B // 32


def along(y, core, sub):
    base = y if sub < 2 else y ^ SLOTS[core][2]
    other = base ^ SLOTS[core][1]
    return jnp.maximum(base, other) if sub % 2 else jnp.minimum(base, other)


def last_kernel(at, own, other, even, odd, total, weights, corner, pieces, whole, t_all, t_right, *scratch):
    x, y, s = at[2], at[1], at[3]
    value = slab_product(at, 4, own, other, even, odd, *scratch)
    for o, tile in enumerate((s, 1 - s)):
        t_all[tile] = total[tile] + value[o * B : (o + 1) * B]
    fill_right(t_right, 0, 0, t_all[...].reshape(2 * B, 2 * B))
    top = product(weights[:B], t_right[...])
    whole[:B] = top[:, :B]
    whole[B : 2 * B] = top[:, B:]
    whole[2 * B :] = product(weights[B:], t_right[:, B:])
    for core in range(2):
        for slot, apart in enumerate(SLOTS[core]):
            p = x ^ apart
            for sub in range(NY):
                start = (core * NX + p) * (NY * N) + along(y, core, sub) * N
                corner[core ^ s, slot, sub] = whole[pl.ds(pl.multiple_of(start, 8), N), :]
            rows = pl.ds(pl.multiple_of((p // 2 * 2 + core) * Q, 8), Q)
            pieces[core ^ s, slot] = t_all[lax.rem(p, 2), rows, :]


def last(place, sigma, other, even, odd, total, weights):
    return pl.pallas_call(
        last_kernel,
        in_specs=[SMEM, VMEM, HBM] + [VMEM] * 4,
        out_specs=[VMEM, VMEM],
        out_shape=[
            jax.ShapeDtypeStruct((2, NX, NY, N, B), F32),
            jax.ShapeDtypeStruct((2, NX, Q, 2 * B), F32),
        ],
        scratch_shapes=[
            pltpu.VMEM((3 * B, B), F32),
            pltpu.VMEM((2, B, 2 * B), F32),
            pltpu.VMEM((WIDE, 2 * B), BF16),
        ]
        + slab_scratch(even),
        compiler_params=params(30),
        cost_estimate=cost(1 << 30, 2 << 20),
        name="last",
    )(place, sigma, other, even, odd, total, weights)


def invert_kernel(_, one_ref, zero_ref, out_one, out_zero, one, zero, sems):
    copies = [pltpu.make_async_copy(one_ref, one, sems.at[0]), pltpu.make_async_copy(zero_ref, zero, sems.at[1])]
    for copy in copies:
        copy.start()
    for copy in copies:
        copy.wait()
    row = lax.broadcasted_iota(jnp.int32, (HALF, HALF), 0)
    col = lax.broadcasted_iota(jnp.int32, (HALF, HALF), 1)
    blocks, inverses = [], []
    for ref in (one, zero):
        for k in range(2):
            block = ref[k * HALF : (k + 1) * HALF, k * HALF : (k + 1) * HALF]
            blocks.append(block)
            inverses.append(jnp.where(row == col, 1.0 / block, 0.0))
    below = jnp.logical_and(row == col + 1, row % 2 == 1)
    scales = [jnp.sum(i, axis=1, keepdims=True) for i in inverses]
    inverses = [
        i - r * jnp.where(below, b, 0.0) * jnp.sum(i, axis=0, keepdims=True)
        for b, i, r in zip(blocks, inverses, scales)
    ]
    size = 2
    while size < HALF:
        below = jnp.logical_and(
            row // (2 * size) == col // (2 * size),
            jnp.logical_and((row // size) % 2 == 1, (col // size) % 2 == 0),
        )
        middles = [exact(jnp.where(below, b, 0.0), i) for b, i in zip(blocks, inverses)]
        inverses = [i - exact(i, m) for i, m in zip(inverses, middles)]
        size *= 2
    for n, (ref, out) in enumerate(((one, out_one), (zero, out_zero))):
        top, bottom = inverses[2 * n], inverses[2 * n + 1]
        out[:HALF, :HALF] = top
        out[HALF:, HALF:] = bottom
        out[:HALF, HALF:] = jnp.zeros((HALF, HALF), F32)
        out[HALF:, :HALF] = -exact(bottom, exact(ref[HALF:, :HALF], top))


def invert(place, one, zero):
    tile = jax.ShapeDtypeStruct((B, B), F32)
    return pl.pallas_call(
        invert_kernel,
        in_specs=[SMEM, HBM, HBM],
        out_specs=[VMEM, VMEM],
        out_shape=[tile, tile],
        scratch_shapes=[pltpu.VMEM((B, B), F32), pltpu.VMEM((B, B), F32), pltpu.SemaphoreType.DMA((2,))],
        compiler_params=params(),
        cost_estimate=cost(1 << 32, 1 << 20),
        name="invert",
    )(place, one, zero)


def constants_kernel(x1_ref, x0_ref, link, z_terms, zt_terms, base):
    x1, x0 = x1_ref[...], x0_ref[...]
    hl = dot3(link[...], x0, NN)
    top = -dot3(x1, hl, NN)
    none = jnp.zeros((B, B), F32)
    for row, column, block in ((0, 0, x1), (0, B, top), (B, 0, none), (B, B, x0)):
        fill_right(z_terms, row, column, block)
        fill_left(zt_terms, column, row, block.T)
    inv1 = dot3(x1, x1, TN)
    cross = dot3(inv1, hl, NN)
    base[:B] = inv1
    base[B : 2 * B] = -cross
    base[2 * B :] = dot3(x0, x0, TN) + dot3(hl, cross, TN)


def constants(x1, x0, link):
    return pl.pallas_call(
        constants_kernel,
        in_specs=[VMEM] * 3,
        out_specs=[VMEM] * 3,
        out_shape=[
            jax.ShapeDtypeStruct((WIDE, 2 * B), BF16),
            jax.ShapeDtypeStruct((2 * B, WIDE), BF16),
            jax.ShapeDtypeStruct((3 * B, B), F32),
        ],
        compiler_params=params(),
        cost_estimate=cost(1 << 29, 3 << 20),
        name="constants",
    )(x1, x0, link)


def weigh_kernel(at, mine, others, weights, rows):
    x, y, s = at[2], at[1], at[3]
    for tile in range(2):
        for g in range(2):
            for core in range(2):
                near = (tile ^ lax.rem(x, 2)) * 2 + (g ^ lax.rem(y, 2))
                start = ((tile * 2 + g) * 2 + core) * Q
                for panel in range(2):
                    block = jnp.where(s == core, mine[near, panel], others[near, panel])
                    rows[start : start + Q, panel * B : (panel + 1) * B] = block
    fill_left(weights, 0, 0, rows[...].T)


def weigh(place, mine, others):
    return pl.pallas_call(
        weigh_kernel,
        in_specs=[SMEM] + [VMEM] * 2,
        out_specs=VMEM,
        out_shape=jax.ShapeDtypeStruct((2 * B, WIDE), BF16),
        scratch_shapes=[pltpu.VMEM((2 * B, 2 * B), F32)],
        compiler_params=params(),
        cost_estimate=cost(1 << 28, 3 << 20),
        name="weigh",
    )(place, mine, others)


def rows_kernel(a, b, z_terms, s1, s0, left):
    fill_left(left, 0, 0, a[...] + b[...])
    both = product(left[...], z_terms[...])
    s1[...] = -both[:, :B]
    s0[...] = -both[:, B:]


def rows(a, b, z_terms):
    out = jax.ShapeDtypeStruct((Q, B), F32)
    return pl.pallas_call(
        rows_kernel,
        in_specs=[VMEM] * 3,
        out_specs=[VMEM] * 2,
        out_shape=[out, out],
        scratch_shapes=[pltpu.VMEM((Q, WIDE), BF16)],
        compiler_params=params(),
        cost_estimate=cost(1 << 27, 2 << 20),
        name="rows",
    )(a, b, z_terms)


def finish_kernel(at, mine, other, z_terms, zt_terms, base, s11, s10, s00, whole, left, right):
    x, y, s = at[2], at[1], at[3]
    for core in range(2):

        def place_all(ref):
            for slot, apart in enumerate(SLOTS[core]):
                for sub in range(NY):
                    start = (core * NX + (x ^ apart)) * (NY * N) + along(y, core, sub) * N
                    whole[pl.ds(pl.multiple_of(start, 8), N), :] = ref[slot, sub // 2, sub % 2]

        @pl.when(s == core)
        def _():
            place_all(mine)

        @pl.when(s != core)
        def _():
            place_all(other)

    crossed = whole[B : 2 * B]
    fill_left(left, 0, 0, whole[:B])
    fill_left(left, 0, B, crossed)
    fill_left(left, B, 0, crossed.T)
    fill_left(left, B, B, whole[2 * B :])
    fill_right(right, 0, 0, product(left[...], z_terms[...]))
    top = product(zt_terms[:B], right[...])
    s11[...] = top[:, :B] + base[:B]
    s10[...] = top[:, B:] + base[B : 2 * B]
    s00[...] = product(zt_terms[B:], right[:, B:]) + base[2 * B :]


def finish(place, mine, other, z_terms, zt_terms, base):
    tile = jax.ShapeDtypeStruct((B, B), F32)
    return pl.pallas_call(
        finish_kernel,
        in_specs=[SMEM] + [VMEM] * 5,
        out_specs=[VMEM] * 3,
        out_shape=[tile, tile, tile],
        scratch_shapes=[
            pltpu.VMEM((3 * B, B), F32),
            pltpu.VMEM((2 * B, WIDE), BF16),
            pltpu.VMEM((WIDE, 2 * B), BF16),
        ],
        compiler_params=params(),
        cost_estimate=cost(1 << 28, 3 << 20),
        name="finish",
    )(place, mine, other, z_terms, zt_terms, base)


def body(sigma, p1, p0, link, diag_one, diag_zero):
    x, y, z, s = (lax.axis_index(name).astype(jnp.int32) for name in ("x", "y", "z", "s"))
    way = 2 * s - 1
    place = jnp.stack([z, y, x, s] + [lax.rem(z + NZ + j * way, NZ) for j in range(5)])

    view = (NZ,) + SLAB
    own = jnp.stack([p1, p0])[None]
    a = jnp.concatenate([own, to_core(own)], axis=0)
    y2 = send(own, lambda x, y, z, s: (x, y + 2, z, s))
    a1 = along_z(a)
    staged = stage(after(place, a), sigma.reshape(view))
    y2 = after(y2, a, staged)
    b = jnp.concatenate([y2, to_core(y2)], axis=0)
    b1 = along_z(b)
    a2 = along_z(after(a1, b))

    sigma_other = to_core(after(sigma, b, a1)).reshape(view)
    even = jnp.concatenate([own, after(y2, a1)], axis=0)
    odd = along_y(even)
    b1, odd = after((b1, odd), b1, odd)
    b2 = along_z(b1)
    z1 = jnp.concatenate([a1, b1], axis=0)
    e1 = along_y(z1)
    pair = jnp.concatenate([own, jnp.where(y % 2 == s, odd[1:], odd[:1])], axis=0)
    a3 = along_z(after(a2, b1))
    crossed = send(after(pair, a2), lambda x, y, z, s: (x ^ 2, y, z, s))

    b2 = after(b2, a2)
    b3 = along_z(b2)
    z2 = jnp.concatenate([a2, b2], axis=0)
    e2 = along_y(z2)
    a3 = after(a3, b2)
    total = multiply(place, 0, staged, sigma_other, even, odd)

    b3, crossed = after((b3, crossed), b3, crossed, a3, total)
    z4 = along_z(jnp.concatenate([a3[:1], b3[:1]], axis=0))
    z3 = jnp.concatenate([a3, b3], axis=0)
    e3 = along_y(z3)
    first = jnp.where(x // 2 == y % 2, pair, crossed)
    second = send(first, lambda x, y, z, s: (x ^ 1, y, z, s))
    total = multiply(place, 1, staged, sigma_other, z1, e1, total)

    z4, second, e2 = after((z4, second, e2), z4, second, e2, total)
    e4 = along_y(z4)
    mine = jnp.concatenate([first, second], axis=0)
    others = to_core(mine)
    total = multiply(place, 2, staged, sigma_other, z2, e2, total)
    weights = weigh(place, mine, others)
    total = multiply(place, 3, staged, sigma_other, z3, e3, total)
    corner, pieces = last(place, staged, sigma_other, z4, e4, total, weights)

    part = corner[0] + to_core(corner[1])
    came = swap(part[2:], "x", 0)
    q = pieces[0] + to_core(pieces[1])
    x1, x0 = invert(after(place, part), diag_one, diag_zero)
    part = part[:2] + after(came, x1, x0, q)
    part = part.reshape(2, 2, 2, N, B)
    a, b, c = to_second_x(part[1, 0]), to_first_y(part[0, 1]), to_both(part[1, 1])
    z_terms, zt_terms, base = constants(x1, x0, after(link, part))
    part = (part[0, 0] + after(a, base)) + (b + c)
    a, b, c = swap(part, "y", 1), to_pair(part, 1), to_pair_y(part)
    q = q[:2] + swap(q[2:], "x", 0)
    part = after((part + a) + (b + c), q)
    a, b, c = (to_pair(part, far) for far in (2, 4, 6))
    came = swap(q[1], "x", 1)
    part = after((part + a) + (b + c), came)
    s1, s0 = rows(q[0], came, z_terms)
    a, b, c = to_second_x(part), to_first_y(part), to_both(part)
    part = jnp.stack([jnp.stack([part, after(b, s1, s0)]), jnp.stack([a, c])])
    sigmas = send(jnp.stack([s1, s0]), lambda x, y, z, s: (y % 2 * 2 + x % 2, y // 2 * 2 + x // 2, z, s))
    mine = after(jnp.concatenate([part, swap(part, "x", 0)], axis=0), sigmas)
    s11, s10, s00 = finish(place, mine, to_core(mine), z_terms, zt_terms, base)
    return sigmas[0], s11, sigmas[1], s10, s00


def solution(mesh):
    mesh = Mesh(mesh.devices.reshape(NX, NZ, NY, 2), AXES)
    in_specs = (P("x", AXES[1:]), P(AXES, None), P(AXES, None), P(), P(), P())
    out_specs = (P(AXES, None), P(), P(AXES, None), P(), P())
    return jax.shard_map(body, mesh=mesh, in_specs=in_specs, out_specs=out_specs, check_vma=False)
```

```python
import jax
import jax.numpy as jnp
from jax import lax
from jax.experimental import pallas as pl
from jax.experimental.pallas import tpu as pltpu
from jax.sharding import Mesh, PartitionSpec as P

F32 = jnp.float32
BF16 = jnp.bfloat16
AXES = ("x", "z", "y", "s")
NX, NY, NZ = 4, 4, 8
B = 256
Q = 64
HALF = 128


def device(x, y, z, s):
    return (x % NX) * 64 + (z % NZ) * 8 + (y % NY) * 2 + s


def send(block, move):
    pairs = [
        (device(x, y, z, s), device(*move(x, y, z, s)))
        for x in range(NX)
        for z in range(NZ)
        for y in range(NY)
        for s in range(2)
    ]
    return lax.ppermute(block, AXES, pairs)


def to_core(block):
    return send(block, lambda x, y, z, s: (x, y, z, 1 - s))


def along_y(block):
    return send(block, lambda x, y, z, s: (x, y + 1 - 2 * s, z, s))


def along_z(block):
    return send(block, lambda x, y, z, s: (x, y, z + 1 - 2 * s, s))


SLOTS = ((0, 3, 1, 2), (0, 1, 3, 2))


def swap(block, axis, turn):
    def move(x, y, z, s):
        apart = SLOTS[s][2 - turn]
        return (x ^ apart, y, z, s) if axis == "x" else (x, y ^ apart, z, s)

    return send(block, move)


def to_pair(block, far):
    return send(block, lambda x, y, z, s: (x, y, ((z + NZ - s) % NZ ^ far) + s, s))


def to_pair_y(block):
    return send(block, lambda x, y, z, s: (x, y ^ SLOTS[s][1], ((z + NZ - s) % NZ ^ 1) + s, s))


def to_second_x(block):
    return swap(block, "x", 1)


def to_first_y(block):
    return swap(block, "y", 0)


def to_both(block):
    return send(block, lambda x, y, z, s: (x ^ SLOTS[s][1], y ^ SLOTS[s][2], z, s))


def after(value, *earlier):
    return lax.optimization_barrier((value, earlier))[0]


def split(value):
    high = value.astype(BF16)
    return high, (value - high.astype(F32)).astype(BF16)


def dot3(left, right, dims):
    lh, ll = split(left)
    rh, rl = split(right)
    d = (dims, ((), ()))
    out = lax.dot_general(lh, rh, d, preferred_element_type=F32)
    out += lax.dot_general(ll, rh, d, preferred_element_type=F32)
    return out + lax.dot_general(lh, rl, d, preferred_element_type=F32)


NN = ((1,), (0,))
TN = ((0,), (0,))


def fill_left(ref, row, place, value):
    deep = ref.shape[1] // 3
    high, low = split(value)
    m, k = value.shape
    ref[row : row + m, place : place + k] = high
    ref[row : row + m, deep + place : deep + place + k] = low
    ref[row : row + m, 2 * deep + place : 2 * deep + place + k] = high


def fill_right(ref, place, column, value):
    deep = ref.shape[0] // 3
    high, low = split(value)
    k, n = value.shape
    ref[place : place + k, column : column + n] = high
    ref[deep + place : deep + place + k, column : column + n] = high
    ref[2 * deep + place : 2 * deep + place + k, column : column + n] = low


def product(left, right):
    return jnp.dot(left, right, preferred_element_type=F32)


def exact(left, right):
    return jnp.dot(left, right, precision=lax.Precision.HIGHEST, preferred_element_type=F32)


def params(limit=16):
    return pltpu.CompilerParams(vmem_limit_bytes=limit * 1024 * 1024)


def cost(flops, moved):
    return pl.CostEstimate(flops=flops, bytes_accessed=moved, transcendentals=0)


VMEM = pl.BlockSpec(memory_space=pltpu.VMEM)
SMEM = pl.BlockSpec(memory_space=pltpu.SMEM)
HBM = pl.BlockSpec(memory_space=pltpu.HBM)
WIDE = 6 * B
SLAB = (NY, 2, Q, B)


def stage(place, sigma):
    def kernel(at, ref, out, sems):
        copies = [pltpu.make_async_copy(ref.at[at[4 + n]], out.at[n], sems.at[n]) for n in range(5)]
        for copy in copies:
            copy.start()
        for copy in copies:
            copy.wait()

    return pl.pallas_call(
        kernel,
        in_specs=[SMEM, HBM],
        out_specs=VMEM,
        out_shape=jax.ShapeDtypeStruct((5,) + SLAB, F32),
        scratch_shapes=[pltpu.SemaphoreType.DMA((5,))],
        compiler_params=params(),
        cost_estimate=cost(0, 5 << 20),
        name="stage",
    )(place, sigma)


def slab_product(at, step, own, other, even, odd, left, right, slabs, sems):
    y, s, slab = at[1], at[3], at[4 + step]
    copy = pltpu.make_async_copy(other.at[slab], slabs, sems.at[0])
    copy.start()
    depth = even.shape[0] * Q
    for n, ref in enumerate((even, odd)):
        for panel in range(2):
            fill_right(right, n * depth, panel * B, ref[:, panel].reshape(depth, B))
    near = lax.rem(y + 3 + 2 * s, NY)
    for o in range(2):
        if o == 1:
            copy.wait()
        for n, first in enumerate((y, near)):
            blocks = [
                (slabs if o else own.at[step])[lax.rem(first + 2 * d, NY), core]
                for d in range(2)
                for core in (s, 1 - s)[: depth // 128]
            ]
            fill_left(left, o * B, n * depth, jnp.concatenate(blocks, axis=0).T)
    return product(left[...], right[...])


def slab_scratch(even):
    deep = 6 * even.shape[0] * Q
    return [
        pltpu.VMEM((2 * B, deep), BF16),
        pltpu.VMEM((deep, 2 * B), BF16),
        pltpu.VMEM(SLAB, F32),
        pltpu.SemaphoreType.DMA((1,)),
    ]


def multiply(place, step, sigma, other, even, odd, total=None):
    totals = [] if total is None else [total]

    def kernel(at, own_ref, other_ref, even_ref, odd_ref, *refs):
        s = at[3]
        out = refs[len(totals)]
        value = slab_product(at, step, own_ref, other_ref, even_ref, odd_ref, *refs[len(totals) + 1 :])
        for o, tile in enumerate((s, 1 - s)):
            part = value[o * B : (o + 1) * B]
            out[tile] = part if total is None else part + refs[0][tile]

    return pl.pallas_call(
        kernel,
        in_specs=[SMEM, VMEM, HBM] + [VMEM] * (2 + len(totals)),
        out_specs=VMEM,
        out_shape=jax.ShapeDtypeStruct((2, B, 2 * B), F32),
        scratch_shapes=slab_scratch(even),
        input_output_aliases={5: 0} if totals else {},
        compiler_params=params(30),
        cost_estimate=cost(3 << 28, 2 << 20),
        name="multiply",
    )(place, sigma, other, even, odd, *totals)


N = 3 * B // 32


def along(y, core, sub):
    base = y if sub < 2 else y ^ SLOTS[core][2]
    other = base ^ SLOTS[core][1]
    return jnp.maximum(base, other) if sub % 2 else jnp.minimum(base, other)


def last_kernel(at, own, other, even, odd, total, weights, corner, pieces, whole, t_all, t_right, *scratch):
    x, y, s = at[2], at[1], at[3]
    value = slab_product(at, 4, own, other, even, odd, *scratch)
    for o, tile in enumerate((s, 1 - s)):
        t_all[tile] = total[tile] + value[o * B : (o + 1) * B]
    fill_right(t_right, 0, 0, t_all[...].reshape(2 * B, 2 * B))
    top = product(weights[:B], t_right[...])
    whole[:B] = top[:, :B]
    whole[B : 2 * B] = top[:, B:]
    whole[2 * B :] = product(weights[B:], t_right[:, B:])
    for core in range(2):
        for slot, apart in enumerate(SLOTS[core]):
            p = x ^ apart
            for sub in range(NY):
                start = (core * NX + p) * (NY * N) + along(y, core, sub) * N
                corner[core ^ s, slot, sub] = whole[pl.ds(pl.multiple_of(start, 8), N), :]
            rows = pl.ds(pl.multiple_of((p // 2 * 2 + core) * Q, 8), Q)
            pieces[core ^ s, slot] = t_all[lax.rem(p, 2), rows, :]


def last(place, sigma, other, even, odd, total, weights):
    return pl.pallas_call(
        last_kernel,
        in_specs=[SMEM, VMEM, HBM] + [VMEM] * 4,
        out_specs=[VMEM, VMEM],
        out_shape=[
            jax.ShapeDtypeStruct((2, NX, NY, N, B), F32),
            jax.ShapeDtypeStruct((2, NX, Q, 2 * B), F32),
        ],
        scratch_shapes=[
            pltpu.VMEM((3 * B, B), F32),
            pltpu.VMEM((2, B, 2 * B), F32),
            pltpu.VMEM((WIDE, 2 * B), BF16),
        ]
        + slab_scratch(even),
        compiler_params=params(30),
        cost_estimate=cost(1 << 30, 2 << 20),
        name="last",
    )(place, sigma, other, even, odd, total, weights)


def invert_kernel(_, one_ref, zero_ref, out_one, out_zero, one, zero, sems):
    copies = [pltpu.make_async_copy(one_ref, one, sems.at[0]), pltpu.make_async_copy(zero_ref, zero, sems.at[1])]
    for copy in copies:
        copy.start()
    for copy in copies:
        copy.wait()
    row = lax.broadcasted_iota(jnp.int32, (HALF, HALF), 0)
    col = lax.broadcasted_iota(jnp.int32, (HALF, HALF), 1)
    blocks, inverses = [], []
    for ref in (one, zero):
        for k in range(2):
            block = ref[k * HALF : (k + 1) * HALF, k * HALF : (k + 1) * HALF]
            blocks.append(block)
            inverses.append(jnp.where(row == col, 1.0 / block, 0.0))
    below = jnp.logical_and(row == col + 1, row % 2 == 1)
    scales = [jnp.sum(i, axis=1, keepdims=True) for i in inverses]
    inverses = [
        i - r * jnp.where(below, b, 0.0) * jnp.sum(i, axis=0, keepdims=True)
        for b, i, r in zip(blocks, inverses, scales)
    ]
    size = 2
    while size < HALF:
        below = jnp.logical_and(
            row // (2 * size) == col // (2 * size),
            jnp.logical_and((row // size) % 2 == 1, (col // size) % 2 == 0),
        )
        middles = [exact(jnp.where(below, b, 0.0), i) for b, i in zip(blocks, inverses)]
        inverses = [i - exact(i, m) for i, m in zip(inverses, middles)]
        size *= 2
    for n, (ref, out) in enumerate(((one, out_one), (zero, out_zero))):
        top, bottom = inverses[2 * n], inverses[2 * n + 1]
        out[:HALF, :HALF] = top
        out[HALF:, HALF:] = bottom
        out[:HALF, HALF:] = jnp.zeros((HALF, HALF), F32)
        out[HALF:, :HALF] = -exact(bottom, exact(ref[HALF:, :HALF], top))


def invert(place, one, zero):
    tile = jax.ShapeDtypeStruct((B, B), F32)
    return pl.pallas_call(
        invert_kernel,
        in_specs=[SMEM, HBM, HBM],
        out_specs=[VMEM, VMEM],
        out_shape=[tile, tile],
        scratch_shapes=[pltpu.VMEM((B, B), F32), pltpu.VMEM((B, B), F32), pltpu.SemaphoreType.DMA((2,))],
        compiler_params=params(),
        cost_estimate=cost(1 << 32, 1 << 20),
        name="invert",
    )(place, one, zero)


def constants_kernel(x1_ref, x0_ref, link, z_terms, zt_terms, base):
    x1, x0 = x1_ref[...], x0_ref[...]
    hl = dot3(link[...], x0, NN)
    top = -dot3(x1, hl, NN)
    none = jnp.zeros((B, B), F32)
    for row, column, block in ((0, 0, x1), (0, B, top), (B, 0, none), (B, B, x0)):
        fill_right(z_terms, row, column, block)
        fill_left(zt_terms, column, row, block.T)
    inv1 = dot3(x1, x1, TN)
    cross = dot3(inv1, hl, NN)
    base[:B] = inv1
    base[B : 2 * B] = -cross
    base[2 * B :] = dot3(x0, x0, TN) + dot3(hl, cross, TN)


def constants(x1, x0, link):
    return pl.pallas_call(
        constants_kernel,
        in_specs=[VMEM] * 3,
        out_specs=[VMEM] * 3,
        out_shape=[
            jax.ShapeDtypeStruct((WIDE, 2 * B), BF16),
            jax.ShapeDtypeStruct((2 * B, WIDE), BF16),
            jax.ShapeDtypeStruct((3 * B, B), F32),
        ],
        compiler_params=params(),
        cost_estimate=cost(1 << 29, 3 << 20),
        name="constants",
    )(x1, x0, link)


def weigh_kernel(at, mine, others, weights, rows):
    x, y, s = at[2], at[1], at[3]
    for tile in range(2):
        for g in range(2):
            for core in range(2):
                near = (tile ^ lax.rem(x, 2)) * 2 + (g ^ lax.rem(y, 2))
                start = ((tile * 2 + g) * 2 + core) * Q
                for panel in range(2):
                    block = jnp.where(s == core, mine[near, panel], others[near, panel])
                    rows[start : start + Q, panel * B : (panel + 1) * B] = block
    fill_left(weights, 0, 0, rows[...].T)


def weigh(place, mine, others):
    return pl.pallas_call(
        weigh_kernel,
        in_specs=[SMEM] + [VMEM] * 2,
        out_specs=VMEM,
        out_shape=jax.ShapeDtypeStruct((2 * B, WIDE), BF16),
        scratch_shapes=[pltpu.VMEM((2 * B, 2 * B), F32)],
        compiler_params=params(),
        cost_estimate=cost(1 << 28, 3 << 20),
        name="weigh",
    )(place, mine, others)


def rows_kernel(a, b, z_terms, s1, s0, left):
    fill_left(left, 0, 0, a[...] + b[...])
    both = product(left[...], z_terms[...])
    s1[...] = -both[:, :B]
    s0[...] = -both[:, B:]


def rows(a, b, z_terms):
    out = jax.ShapeDtypeStruct((Q, B), F32)
    return pl.pallas_call(
        rows_kernel,
        in_specs=[VMEM] * 3,
        out_specs=[VMEM] * 2,
        out_shape=[out, out],
        scratch_shapes=[pltpu.VMEM((Q, WIDE), BF16)],
        compiler_params=params(),
        cost_estimate=cost(1 << 27, 2 << 20),
        name="rows",
    )(a, b, z_terms)


def finish_kernel(at, mine, other, z_terms, zt_terms, base, s11, s10, s00, whole, left, right):
    x, y, s = at[2], at[1], at[3]
    for core in range(2):

        def place_all(ref):
            for slot, apart in enumerate(SLOTS[core]):
                for sub in range(NY):
                    start = (core * NX + (x ^ apart)) * (NY * N) + along(y, core, sub) * N
                    whole[pl.ds(pl.multiple_of(start, 8), N), :] = ref[slot, sub // 2, sub % 2]

        @pl.when(s == core)
        def _():
            place_all(mine)

        @pl.when(s != core)
        def _():
            place_all(other)

    crossed = whole[B : 2 * B]
    fill_left(left, 0, 0, whole[:B])
    fill_left(left, 0, B, crossed)
    fill_left(left, B, 0, crossed.T)
    fill_left(left, B, B, whole[2 * B :])
    fill_right(right, 0, 0, product(left[...], z_terms[...]))
    top = product(zt_terms[:B], right[...])
    s11[...] = top[:, :B] + base[:B]
    s10[...] = top[:, B:] + base[B : 2 * B]
    s00[...] = product(zt_terms[B:], right[:, B:]) + base[2 * B :]


def finish(place, mine, other, z_terms, zt_terms, base):
    tile = jax.ShapeDtypeStruct((B, B), F32)
    return pl.pallas_call(
        finish_kernel,
        in_specs=[SMEM] + [VMEM] * 5,
        out_specs=[VMEM] * 3,
        out_shape=[tile, tile, tile],
        scratch_shapes=[
            pltpu.VMEM((3 * B, B), F32),
            pltpu.VMEM((2 * B, WIDE), BF16),
            pltpu.VMEM((WIDE, 2 * B), BF16),
        ],
        compiler_params=params(),
        cost_estimate=cost(1 << 28, 3 << 20),
        name="finish",
    )(place, mine, other, z_terms, zt_terms, base)


def body(sigma, p1, p0, link, diag_one, diag_zero):
    x, y, z, s = (lax.axis_index(name).astype(jnp.int32) for name in ("x", "y", "z", "s"))
    way = 2 * s - 1
    place = jnp.stack([z, y, x, s] + [lax.rem(z + NZ + j * way, NZ) for j in range(5)])

    view = (NZ,) + SLAB
    own = jnp.stack([p1, p0])[None]
    a = jnp.concatenate([own, to_core(own)], axis=0)
    y2 = send(own, lambda x, y, z, s: (x, y + 2, z, s))
    a1 = along_z(a)
    staged = stage(after(place, a), sigma.reshape(view))
    y2 = after(y2, a, staged)
    b = jnp.concatenate([y2, to_core(y2)], axis=0)
    b1 = along_z(b)
    a2 = along_z(after(a1, b))

    sigma_other = to_core(after(sigma, b, a1)).reshape(view)
    even = jnp.concatenate([own, after(y2, a1)], axis=0)
    odd = along_y(even)
    b1, odd = after((b1, odd), b1, odd)
    b2 = along_z(b1)
    z1 = jnp.concatenate([a1, b1], axis=0)
    e1 = along_y(z1)
    pair = jnp.concatenate([own, jnp.where(y % 2 == s, odd[1:], odd[:1])], axis=0)
    a3 = along_z(after(a2, b1))
    crossed = send(after(pair, a2), lambda x, y, z, s: (x ^ 2, y, z, s))

    b2 = after(b2, a2)
    b3 = along_z(b2)
    z2 = jnp.concatenate([a2, b2], axis=0)
    e2 = along_y(z2)
    a3 = after(a3, b2)
    total = multiply(place, 0, staged, sigma_other, even, odd)

    b3, crossed = after((b3, crossed), b3, crossed, a3, total)
    z4 = along_z(jnp.concatenate([a3[:1], b3[:1]], axis=0))
    z3 = jnp.concatenate([a3, b3], axis=0)
    e3 = along_y(z3)
    first = jnp.where(x // 2 == y % 2, pair, crossed)
    second = send(first, lambda x, y, z, s: (x ^ 1, y, z, s))
    total = multiply(place, 1, staged, sigma_other, z1, e1, total)

    z4, second, e2 = after((z4, second, e2), z4, second, e2, total)
    e4 = along_y(z4)
    mine = jnp.concatenate([first, second], axis=0)
    others = to_core(mine)
    total = multiply(place, 2, staged, sigma_other, z2, e2, total)
    weights = weigh(place, mine, others)
    total = multiply(place, 3, staged, sigma_other, z3, e3, total)
    corner, pieces = last(place, staged, sigma_other, z4, e4, total, weights)

    part = corner[0] + to_core(corner[1])
    came = swap(part[2:], "x", 0)
    q = pieces[0] + to_core(pieces[1])
    x1, x0 = invert(after(place, part), diag_one, diag_zero)
    part = part[:2] + after(came, x1, x0, q)
    part = part.reshape(2, 2, 2, N, B)
    a, b, c = to_second_x(part[1, 0]), to_first_y(part[0, 1]), to_both(part[1, 1])
    z_terms, zt_terms, base = constants(x1, x0, after(link, part))
    part = (part[0, 0] + after(a, base)) + (b + c)
    got = swap(q[2:], "x", 0)
    a, b, c = swap(part, "y", 1), to_pair(part, 1), to_pair_y(after(part, got))
    q = q[:2] + got
    part = (part + a) + (b + c)
    got = swap(q[1], "x", 1)
    a, b, c = to_pair(part, 2), to_pair(part, 4), to_pair(after(part, got), 6)
    part = (part + a) + (b + c)
    s1, s0 = rows(q[0], got, z_terms)
    sigmas = send(jnp.stack([s1, s0]), lambda x, y, z, s: (y % 2 * 2 + x % 2, y // 2 * 2 + x // 2, z, s))
    a, b, c = to_second_x(part), to_first_y(part), to_both(after(part, sigmas))
    part = jnp.stack([jnp.stack([part, b]), jnp.stack([a, c])])
    mine = jnp.concatenate([part, swap(part, "x", 0)], axis=0)
    s11, s10, s00 = finish(place, mine, to_core(mine), z_terms, zt_terms, base)
    return sigmas[0], s11, sigmas[1], s10, s00


def solution(mesh):
    mesh = Mesh(mesh.devices.reshape(NX, NZ, NY, 2), AXES)
    in_specs = (P("x", AXES[1:]), P(AXES, None), P(AXES, None), P(), P(), P())
    out_specs = (P(AXES, None), P(), P(AXES, None), P(), P())
    return jax.shard_map(body, mesh=mesh, in_specs=in_specs, out_specs=out_specs, check_vma=False)
```

```python
import jax
import jax.numpy as jnp
from jax import lax
from jax.experimental import pallas as pl
from jax.experimental.pallas import tpu as pltpu
from jax.sharding import Mesh, PartitionSpec as P

F32 = jnp.float32
BF16 = jnp.bfloat16
AXES = ("x", "z", "y", "s")
NX, NY, NZ = 4, 4, 8
B = 256
Q = 64
HALF = 128


def device(x, y, z, s):
    return (x % NX) * 64 + (z % NZ) * 8 + (y % NY) * 2 + s


def send(block, move):
    pairs = [
        (device(x, y, z, s), device(*move(x, y, z, s)))
        for x in range(NX)
        for z in range(NZ)
        for y in range(NY)
        for s in range(2)
    ]
    return lax.ppermute(block, AXES, pairs)


def to_core(block):
    return send(block, lambda x, y, z, s: (x, y, z, 1 - s))


def along_y(block):
    return send(block, lambda x, y, z, s: (x, y + 1 - 2 * s, z, s))


def along_z(block):
    return send(block, lambda x, y, z, s: (x, y, z + 1 - 2 * s, s))


SLOTS = ((0, 3, 1, 2), (0, 1, 3, 2))


def swap(block, axis, turn):
    def move(x, y, z, s):
        apart = SLOTS[s][2 - turn]
        return (x ^ apart, y, z, s) if axis == "x" else (x, y ^ apart, z, s)

    return send(block, move)


def to_pair(block, far):
    return send(block, lambda x, y, z, s: (x, y, ((z + NZ - s) % NZ ^ far) + s, s))


def to_pair_y(block):
    return send(block, lambda x, y, z, s: (x, y ^ SLOTS[s][1], ((z + NZ - s) % NZ ^ 1) + s, s))


def to_second_x(block):
    return swap(block, "x", 1)


def to_first_y(block):
    return swap(block, "y", 0)


def to_both(block):
    return send(block, lambda x, y, z, s: (x ^ SLOTS[s][1], y ^ SLOTS[s][2], z, s))


def after(value, *earlier):
    return lax.optimization_barrier((value, earlier))[0]


def split(value):
    high = value.astype(BF16)
    return high, (value - high.astype(F32)).astype(BF16)


def dot3(left, right, dims):
    lh, ll = split(left)
    rh, rl = split(right)
    d = (dims, ((), ()))
    out = lax.dot_general(lh, rh, d, preferred_element_type=F32)
    out += lax.dot_general(ll, rh, d, preferred_element_type=F32)
    return out + lax.dot_general(lh, rl, d, preferred_element_type=F32)


NN = ((1,), (0,))
TN = ((0,), (0,))


def fill_left(ref, row, place, value):
    deep = ref.shape[1] // 3
    high, low = split(value)
    m, k = value.shape
    ref[row : row + m, place : place + k] = high
    ref[row : row + m, deep + place : deep + place + k] = low
    ref[row : row + m, 2 * deep + place : 2 * deep + place + k] = high


def fill_right(ref, place, column, value):
    deep = ref.shape[0] // 3
    high, low = split(value)
    k, n = value.shape
    ref[place : place + k, column : column + n] = high
    ref[deep + place : deep + place + k, column : column + n] = high
    ref[2 * deep + place : 2 * deep + place + k, column : column + n] = low


def product(left, right):
    return jnp.dot(left, right, preferred_element_type=F32)


def half_product(left, right, columns):
    return sum(product(left[:B, n : n + B], right[n : n + B, columns]) for n in range(0, WIDE, 2 * B))


def exact(left, right):
    return jnp.dot(left, right, precision=lax.Precision.HIGHEST, preferred_element_type=F32)


def params(limit=10):
    return pltpu.CompilerParams(vmem_limit_bytes=limit * 1024 * 1024)


def cost(flops, moved):
    return pl.CostEstimate(flops=flops, bytes_accessed=moved, transcendentals=0)


VMEM = pl.BlockSpec(memory_space=pltpu.VMEM)
SMEM = pl.BlockSpec(memory_space=pltpu.SMEM)
HBM = pl.BlockSpec(memory_space=pltpu.HBM)
WIDE = 6 * B
SLAB = (NY, 2, Q, B)


def stage(place, sigma):
    def kernel(at, ref, out, sems):
        copies = [pltpu.make_async_copy(ref.at[at[4 + n]], out.at[n], sems.at[n]) for n in range(5)]
        for copy in copies:
            copy.start()
        for copy in copies:
            copy.wait()

    return pl.pallas_call(
        kernel,
        in_specs=[SMEM, HBM],
        out_specs=VMEM,
        out_shape=jax.ShapeDtypeStruct((5,) + SLAB, F32),
        scratch_shapes=[pltpu.SemaphoreType.DMA((5,))],
        compiler_params=params(4),
        cost_estimate=cost(0, 5 << 20),
        name="stage",
    )(place, sigma)


def slab_product(at, step, own, other, even, odd, left, right, slabs, sems):
    y, s, slab = at[1], at[3], at[4 + step]
    copy = pltpu.make_async_copy(other.at[slab], slabs, sems.at[0])
    copy.start()
    depth = even.shape[0] * Q
    for n, ref in enumerate((even, odd)):
        for panel in range(2):
            fill_right(right, n * depth, panel * B, ref[:, panel].reshape(depth, B))
    near = lax.rem(y + 3 + 2 * s, NY)
    for o in range(2):
        if o == 1:
            copy.wait()
        for n, first in enumerate((y, near)):
            blocks = [
                (slabs if o else own.at[step])[lax.rem(first + 2 * d, NY), core]
                for d in range(2)
                for core in (s, 1 - s)[: depth // 128]
            ]
            fill_left(left, o * B, n * depth, jnp.concatenate(blocks, axis=0).T)
    return product(left[...], right[...])


def slab_scratch(even):
    deep = 6 * even.shape[0] * Q
    return [
        pltpu.VMEM((2 * B, deep), BF16),
        pltpu.VMEM((deep, 2 * B), BF16),
        pltpu.VMEM(SLAB, F32),
        pltpu.SemaphoreType.DMA((1,)),
    ]


def multiply(place, step, sigma, other, even, odd, total=None):
    totals = [] if total is None else [total]

    def kernel(at, own_ref, other_ref, even_ref, odd_ref, *refs):
        s = at[3]
        out = refs[len(totals)]
        value = slab_product(at, step, own_ref, other_ref, even_ref, odd_ref, *refs[len(totals) + 1 :])
        for o, tile in enumerate((s, 1 - s)):
            part = value[o * B : (o + 1) * B]
            out[tile] = part if total is None else part + refs[0][tile]

    return pl.pallas_call(
        kernel,
        in_specs=[SMEM, VMEM, HBM] + [VMEM] * (2 + len(totals)),
        out_specs=VMEM,
        out_shape=jax.ShapeDtypeStruct((2, B, 2 * B), F32),
        scratch_shapes=slab_scratch(even),
        input_output_aliases={5: 0} if totals else {},
        compiler_params=params(12),
        cost_estimate=cost(3 << 28, 2 << 20),
        name="multiply",
    )(place, sigma, other, even, odd, *totals)


N = 3 * B // 32


def along(y, core, sub):
    base = y if sub < 2 else y ^ SLOTS[core][2]
    other = base ^ SLOTS[core][1]
    return jnp.maximum(base, other) if sub % 2 else jnp.minimum(base, other)


def last_kernel(at, own, other, even, odd, total, weights, corner, pieces, whole, t_all, t_right, *scratch):
    x, y, s = at[2], at[1], at[3]
    value = slab_product(at, 4, own, other, even, odd, *scratch)
    for o, tile in enumerate((s, 1 - s)):
        t_all[tile] = total[tile] + value[o * B : (o + 1) * B]
    fill_right(t_right, 0, 0, t_all[...].reshape(2 * B, 2 * B))
    top = product(weights[:B], t_right[...])
    whole[:B] = top[:, :B]
    whole[B : 2 * B] = top[:, B:]
    whole[2 * B :] = product(weights[B:], t_right[:, B:])
    for core in range(2):
        for slot, apart in enumerate(SLOTS[core]):
            p = x ^ apart
            for sub in range(NY):
                start = (core * NX + p) * (NY * N) + along(y, core, sub) * N
                corner[core ^ s, slot, sub] = whole[pl.ds(pl.multiple_of(start, 8), N), :]
            rows = pl.ds(pl.multiple_of((p // 2 * 2 + core) * Q, 8), Q)
            pieces[core ^ s, slot] = t_all[lax.rem(p, 2), rows, :]


def last(place, sigma, other, even, odd, total, weights):
    return pl.pallas_call(
        last_kernel,
        in_specs=[SMEM, VMEM, HBM] + [VMEM] * 4,
        out_specs=[VMEM, VMEM],
        out_shape=[
            jax.ShapeDtypeStruct((2, NX, NY, N, B), F32),
            jax.ShapeDtypeStruct((2, NX, Q, 2 * B), F32),
        ],
        scratch_shapes=[
            pltpu.VMEM((3 * B, B), F32),
            pltpu.VMEM((2, B, 2 * B), F32),
            pltpu.VMEM((WIDE, 2 * B), BF16),
        ]
        + slab_scratch(even),
        compiler_params=params(20),
        cost_estimate=cost(1 << 30, 2 << 20),
        name="last",
    )(place, sigma, other, even, odd, total, weights)


def invert_kernel(_, one_ref, zero_ref, out_one, out_zero, one, zero, sems):
    copies = [pltpu.make_async_copy(one_ref, one, sems.at[0]), pltpu.make_async_copy(zero_ref, zero, sems.at[1])]
    for copy in copies:
        copy.start()
    for copy in copies:
        copy.wait()
    row = lax.broadcasted_iota(jnp.int32, (HALF, HALF), 0)
    col = lax.broadcasted_iota(jnp.int32, (HALF, HALF), 1)
    blocks, inverses = [], []
    for ref in (one, zero):
        for k in range(2):
            block = ref[k * HALF : (k + 1) * HALF, k * HALF : (k + 1) * HALF]
            blocks.append(block)
            inverses.append(jnp.where(row == col, 1.0 / block, 0.0))
    below = jnp.logical_and(row == col + 1, row % 2 == 1)
    scales = [jnp.sum(i, axis=1, keepdims=True) for i in inverses]
    inverses = [
        i - r * jnp.where(below, b, 0.0) * jnp.sum(i, axis=0, keepdims=True)
        for b, i, r in zip(blocks, inverses, scales)
    ]
    size = 2
    while size < HALF:
        below = jnp.logical_and(
            row // (2 * size) == col // (2 * size),
            jnp.logical_and((row // size) % 2 == 1, (col // size) % 2 == 0),
        )
        middles = [exact(jnp.where(below, b, 0.0), i) for b, i in zip(blocks, inverses)]
        inverses = [i - exact(i, m) for i, m in zip(inverses, middles)]
        size *= 2
    for n, (ref, out) in enumerate(((one, out_one), (zero, out_zero))):
        top, bottom = inverses[2 * n], inverses[2 * n + 1]
        out[:HALF, :HALF] = top
        out[HALF:, HALF:] = bottom
        out[:HALF, HALF:] = jnp.zeros((HALF, HALF), F32)
        out[HALF:, :HALF] = -exact(bottom, exact(ref[HALF:, :HALF], top))


def invert(place, one, zero):
    tile = jax.ShapeDtypeStruct((B, B), F32)
    return pl.pallas_call(
        invert_kernel,
        in_specs=[SMEM, HBM, HBM],
        out_specs=[VMEM, VMEM],
        out_shape=[tile, tile],
        scratch_shapes=[pltpu.VMEM((B, B), F32), pltpu.VMEM((B, B), F32), pltpu.SemaphoreType.DMA((2,))],
        compiler_params=params(),
        cost_estimate=cost(1 << 32, 1 << 20),
        name="invert",
    )(place, one, zero)


def constants_kernel(x1_ref, x0_ref, link, z_terms, zt_terms, base):
    x1, x0 = x1_ref[...], x0_ref[...]
    hl = dot3(link[...], x0, NN)
    top = -dot3(x1, hl, NN)
    none = jnp.zeros((B, B), F32)
    for row, column, block in ((0, 0, x1), (0, B, top), (B, 0, none), (B, B, x0)):
        fill_right(z_terms, row, column, block)
        fill_left(zt_terms, column, row, block.T)
    inv1 = dot3(x1, x1, TN)
    cross = dot3(inv1, hl, NN)
    base[:B] = inv1
    base[B : 2 * B] = -cross
    base[2 * B :] = dot3(x0, x0, TN) + dot3(hl, cross, TN)


def constants(x1, x0, link):
    return pl.pallas_call(
        constants_kernel,
        in_specs=[VMEM] * 3,
        out_specs=[VMEM] * 3,
        out_shape=[
            jax.ShapeDtypeStruct((WIDE, 2 * B), BF16),
            jax.ShapeDtypeStruct((2 * B, WIDE), BF16),
            jax.ShapeDtypeStruct((3 * B, B), F32),
        ],
        compiler_params=params(),
        cost_estimate=cost(1 << 29, 3 << 20),
        name="constants",
    )(x1, x0, link)


def weigh_kernel(at, mine, others, weights, rows):
    x, y, s = at[2], at[1], at[3]
    for tile in range(2):
        for g in range(2):
            for core in range(2):
                near = (tile ^ lax.rem(x, 2)) * 2 + (g ^ lax.rem(y, 2))
                start = ((tile * 2 + g) * 2 + core) * Q
                for panel in range(2):
                    block = jnp.where(s == core, mine[near, panel], others[near, panel])
                    rows[start : start + Q, panel * B : (panel + 1) * B] = block
    fill_left(weights, 0, 0, rows[...].T)


def weigh(place, mine, others):
    return pl.pallas_call(
        weigh_kernel,
        in_specs=[SMEM] + [VMEM] * 2,
        out_specs=VMEM,
        out_shape=jax.ShapeDtypeStruct((2 * B, WIDE), BF16),
        scratch_shapes=[pltpu.VMEM((2 * B, 2 * B), F32)],
        compiler_params=params(),
        cost_estimate=cost(1 << 28, 3 << 20),
        name="weigh",
    )(place, mine, others)


def rows_kernel(a, b, z_terms, s1, s0, left):
    fill_left(left, 0, 0, a[...] + b[...])
    both = product(left[...], z_terms[...])
    s1[...] = -both[:, :B]
    s0[...] = -both[:, B:]


def rows(a, b, z_terms):
    out = jax.ShapeDtypeStruct((Q, B), F32)
    return pl.pallas_call(
        rows_kernel,
        in_specs=[VMEM] * 3,
        out_specs=[VMEM] * 2,
        out_shape=[out, out],
        scratch_shapes=[pltpu.VMEM((Q, WIDE), BF16)],
        compiler_params=params(),
        cost_estimate=cost(1 << 27, 2 << 20),
        name="rows",
    )(a, b, z_terms)


def finish_kernel(at, mine, other, z_terms, zt_terms, base, s11, s10, s00, whole, left, right):
    x, y, s = at[2], at[1], at[3]
    for core in range(2):

        def place_all(ref):
            for slot, apart in enumerate(SLOTS[core]):
                for sub in range(NY):
                    start = (core * NX + (x ^ apart)) * (NY * N) + along(y, core, sub) * N
                    whole[pl.ds(pl.multiple_of(start, 8), N), :] = ref[slot, sub // 2, sub % 2]

        @pl.when(s == core)
        def _():
            place_all(mine)

        @pl.when(s != core)
        def _():
            place_all(other)

    crossed = whole[B : 2 * B]
    fill_left(left, 0, 0, whole[:B])
    fill_left(left, 0, B, crossed)
    fill_left(left, B, 0, crossed.T)
    fill_left(left, B, B, whole[2 * B :])
    fill_right(right, 0, 0, half_product(left, z_terms, slice(0, B)))
    fill_right(right, 0, B, product(left[...], z_terms[:, B:]))
    top = half_product(zt_terms, right, slice(0, 2 * B))
    s11[...] = top[:, :B] + base[:B]
    s10[...] = top[:, B:] + base[B : 2 * B]
    s00[...] = product(zt_terms[B:], right[:, B:]) + base[2 * B :]


def finish(place, mine, other, z_terms, zt_terms, base):
    tile = jax.ShapeDtypeStruct((B, B), F32)
    return pl.pallas_call(
        finish_kernel,
        in_specs=[SMEM] + [VMEM] * 5,
        out_specs=[VMEM] * 3,
        out_shape=[tile, tile, tile],
        scratch_shapes=[
            pltpu.VMEM((3 * B, B), F32),
            pltpu.VMEM((2 * B, WIDE), BF16),
            pltpu.VMEM((WIDE, 2 * B), BF16),
        ],
        compiler_params=params(),
        cost_estimate=cost(1 << 28, 3 << 20),
        name="finish",
    )(place, mine, other, z_terms, zt_terms, base)


def body(sigma, p1, p0, link, diag_one, diag_zero):
    x, y, z, s = (lax.axis_index(name).astype(jnp.int32) for name in ("x", "y", "z", "s"))
    way = 2 * s - 1
    place = jnp.stack([z, y, x, s] + [lax.rem(z + NZ + j * way, NZ) for j in range(5)])

    view = (NZ,) + SLAB
    own = jnp.stack([p1, p0])[None]
    a = jnp.concatenate([own, to_core(own)], axis=0)
    y2 = send(own, lambda x, y, z, s: (x, y + 2, z, s))
    a1 = along_z(a)
    staged = stage(after(place, a), sigma.reshape(view))
    y2 = after(y2, a, staged)
    b = jnp.concatenate([y2, to_core(y2)], axis=0)
    b1 = along_z(b)
    a2 = along_z(after(a1, b))

    sigma_other = to_core(after(sigma, b, a1)).reshape(view)
    even = jnp.concatenate([own, after(y2, a1)], axis=0)
    odd = along_y(even)
    b1, odd = after((b1, odd), b1, odd)
    b2 = along_z(b1)
    z1 = jnp.concatenate([a1, b1], axis=0)
    e1 = along_y(z1)
    pair = jnp.concatenate([own, jnp.where(y % 2 == s, odd[1:], odd[:1])], axis=0)
    a3 = along_z(after(a2, b1))
    crossed = send(after(pair, a2), lambda x, y, z, s: (x ^ 2, y, z, s))

    b2 = after(b2, a2)
    b3 = along_z(b2)
    z2 = jnp.concatenate([a2, b2], axis=0)
    e2 = along_y(z2)
    a3 = after(a3, b2)
    total = multiply(place, 0, staged, sigma_other, even, odd)

    b3, crossed = after((b3, crossed), b3, crossed, a3, total)
    z4 = along_z(jnp.concatenate([a3[:1], b3[:1]], axis=0))
    z3 = jnp.concatenate([a3, b3], axis=0)
    e3 = along_y(z3)
    first = jnp.where(x // 2 == y % 2, pair, crossed)
    second = send(first, lambda x, y, z, s: (x ^ 1, y, z, s))
    total = multiply(place, 1, staged, sigma_other, z1, e1, total)

    z4, second, e2 = after((z4, second, e2), z4, second, e2, total)
    e4 = along_y(z4)
    mine = jnp.concatenate([first, second], axis=0)
    others = to_core(mine)
    total = multiply(place, 2, staged, sigma_other, z2, e2, total)
    weights = weigh(place, mine, others)
    total = multiply(place, 3, staged, sigma_other, z3, e3, total)
    corner, pieces = last(place, staged, sigma_other, z4, e4, total, weights)

    part = corner[0] + to_core(corner[1])
    came = swap(part[2:], "x", 0)
    q = pieces[0] + to_core(pieces[1])
    x1, x0 = invert(after(place, part), diag_one, diag_zero)
    part = part[:2] + after(came, x1, x0, q)
    part = part.reshape(2, 2, 2, N, B)
    a, b, c = to_second_x(part[1, 0]), to_first_y(part[0, 1]), to_both(part[1, 1])
    z_terms, zt_terms, base = constants(x1, x0, after(link, part))
    part = (part[0, 0] + after(a, base)) + (b + c)
    got = swap(q[2:], "x", 0)
    a, b, c = swap(part, "y", 1), to_pair(part, 1), to_pair_y(after(part, got))
    q = q[:2] + got
    part = (part + a) + (b + c)
    got = swap(q[1], "x", 1)
    a, b, c = to_pair(part, 2), to_pair(part, 4), to_pair(after(part, got), 6)
    part = (part + a) + (b + c)
    s1, s0 = rows(q[0], got, z_terms)
    sigmas = send(jnp.stack([s1, s0]), lambda x, y, z, s: (y % 2 * 2 + x % 2, y // 2 * 2 + x // 2, z, s))
    a, b, c = to_second_x(part), to_first_y(part), to_both(after(part, sigmas))
    part = jnp.stack([jnp.stack([part, b]), jnp.stack([a, c])])
    mine = jnp.concatenate([part, swap(part, "x", 0)], axis=0)
    s11, s10, s00 = finish(place, mine, to_core(mine), z_terms, zt_terms, base)
    return sigmas[0], s11, sigmas[1], s10, s00


def solution(mesh):
    mesh = Mesh(mesh.devices.reshape(NX, NZ, NY, 2), AXES)
    in_specs = (P("x", AXES[1:]), P(AXES, None), P(AXES, None), P(), P(), P())
    out_specs = (P(AXES, None), P(), P(AXES, None), P(), P())
    return jax.shard_map(body, mesh=mesh, in_specs=in_specs, out_specs=out_specs, check_vma=False)
```

```python
import jax
import jax.numpy as jnp
from jax import lax
from jax.experimental import pallas as pl
from jax.experimental.pallas import tpu as pltpu
from jax.sharding import Mesh, PartitionSpec as P

F32 = jnp.float32
BF16 = jnp.bfloat16
AXES = ("x", "z", "y", "s")
NX, NY, NZ = 4, 4, 8
B = 256
Q = 64
HALF = 128


def device(x, y, z, s):
    return (x % NX) * 64 + (z % NZ) * 8 + (y % NY) * 2 + s


def send(block, move):
    pairs = [
        (device(x, y, z, s), device(*move(x, y, z, s)))
        for x in range(NX)
        for z in range(NZ)
        for y in range(NY)
        for s in range(2)
    ]
    return lax.ppermute(block, AXES, pairs)


def to_core(block):
    return send(block, lambda x, y, z, s: (x, y, z, 1 - s))


def along_y(block):
    return send(block, lambda x, y, z, s: (x, y + 1 - 2 * s, z, s))


def along_z(block):
    return send(block, lambda x, y, z, s: (x, y, z + 1 - 2 * s, s))


SLOTS = ((0, 3, 1, 2), (0, 1, 3, 2))


def swap(block, axis, turn):
    def move(x, y, z, s):
        apart = SLOTS[s][2 - turn]
        return (x ^ apart, y, z, s) if axis == "x" else (x, y ^ apart, z, s)

    return send(block, move)


def to_pair(block, far):
    return send(block, lambda x, y, z, s: (x, y, ((z + NZ - s) % NZ ^ far) + s, s))


def to_pair_y(block):
    return send(block, lambda x, y, z, s: (x, y ^ SLOTS[s][1], ((z + NZ - s) % NZ ^ 1) + s, s))


def to_second_x(block):
    return swap(block, "x", 1)


def to_first_y(block):
    return swap(block, "y", 0)


def to_both(block):
    return send(block, lambda x, y, z, s: (x ^ SLOTS[s][1], y ^ SLOTS[s][2], z, s))


def after(value, *earlier):
    return lax.optimization_barrier((value, earlier))[0]


def split(value):
    high = value.astype(BF16)
    return high, (value - high.astype(F32)).astype(BF16)


def dot3(left, right, dims):
    lh, ll = split(left)
    rh, rl = split(right)
    d = (dims, ((), ()))
    out = lax.dot_general(lh, rh, d, preferred_element_type=F32)
    out += lax.dot_general(ll, rh, d, preferred_element_type=F32)
    return out + lax.dot_general(lh, rl, d, preferred_element_type=F32)


NN = ((1,), (0,))
TN = ((0,), (0,))


def fill_left(ref, row, place, value):
    deep = ref.shape[1] // 3
    high, low = split(value)
    m, k = value.shape
    ref[row : row + m, place : place + k] = high
    ref[row : row + m, deep + place : deep + place + k] = low
    ref[row : row + m, 2 * deep + place : 2 * deep + place + k] = high


def fill_right(ref, place, column, value):
    deep = ref.shape[0] // 3
    high, low = split(value)
    k, n = value.shape
    ref[place : place + k, column : column + n] = high
    ref[deep + place : deep + place + k, column : column + n] = high
    ref[2 * deep + place : 2 * deep + place + k, column : column + n] = low


def product(left, right):
    return jnp.dot(left, right, preferred_element_type=F32)


def half_product(left, right, columns):
    return sum(product(left[:B, n : n + B], right[n : n + B, columns]) for n in range(0, WIDE, 2 * B))


def exact(left, right):
    return jnp.dot(left, right, precision=lax.Precision.HIGHEST, preferred_element_type=F32)


def params(limit=10):
    return pltpu.CompilerParams(vmem_limit_bytes=limit * 1024 * 1024)


def cost(flops, moved):
    return pl.CostEstimate(flops=flops, bytes_accessed=moved, transcendentals=0)


VMEM = pl.BlockSpec(memory_space=pltpu.VMEM)
SMEM = pl.BlockSpec(memory_space=pltpu.SMEM)
HBM = pl.BlockSpec(memory_space=pltpu.HBM)
WIDE = 6 * B
SLAB = (NY, 2, Q, B)


DEPTHS = (B, 2 * B, 2 * B, 2 * B, B)


def fill_slab(at, slab, left, row, depth):
    y, s = at[1], at[3]
    half = depth // 2
    for n, first in enumerate((y, lax.rem(y + 3 + 2 * s, NY))):
        blocks = [slab[lax.rem(first + 2 * d, NY), core] for d in range(2) for core in (s, 1 - s)[: half // 128]]
        fill_left(left, row, n * half, jnp.concatenate(blocks, axis=0).T)


def stage(place, sigma):
    def kernel(at, ref, *refs):
        outs, slabs, sems = refs[:5], refs[5], refs[6]
        copies = [pltpu.make_async_copy(ref.at[at[4 + n]], slabs.at[n], sems.at[n]) for n in range(5)]
        for copy in copies:
            copy.start()
        for n, copy in enumerate(copies):
            copy.wait()
            fill_slab(at, slabs.at[n], outs[n], 0, DEPTHS[n])

    return pl.pallas_call(
        kernel,
        in_specs=[SMEM, HBM],
        out_specs=[VMEM] * 5,
        out_shape=[jax.ShapeDtypeStruct((B, 3 * depth), BF16) for depth in DEPTHS],
        scratch_shapes=[pltpu.VMEM((5,) + SLAB, F32), pltpu.SemaphoreType.DMA((5,))],
        compiler_params=params(12),
        cost_estimate=cost(0, 5 << 20),
        name="stage",
    )(place, sigma)


def slab_product(at, step, own, other, even, odd, left, right, slab, sems):
    copy = pltpu.make_async_copy(other.at[at[4 + step]], slab, sems.at[0])
    copy.start()
    depth = even.shape[0] * Q
    for n, ref in enumerate((even, odd)):
        for panel in range(2):
            fill_right(right, n * depth, panel * B, ref[:, panel].reshape(depth, B))
    left[:B] = own[...]
    copy.wait()
    fill_slab(at, slab, left, B, 2 * depth)
    return product(left[...], right[...])


def slab_scratch(even):
    deep = 6 * even.shape[0] * Q
    return [
        pltpu.VMEM((2 * B, deep), BF16),
        pltpu.VMEM((deep, 2 * B), BF16),
        pltpu.VMEM(SLAB, F32),
        pltpu.SemaphoreType.DMA((1,)),
    ]


def multiply(place, step, sigma, other, even, odd, total=None):
    totals = [] if total is None else [total]

    def kernel(at, own_ref, other_ref, even_ref, odd_ref, *refs):
        s = at[3]
        out = refs[len(totals)]
        value = slab_product(at, step, own_ref, other_ref, even_ref, odd_ref, *refs[len(totals) + 1 :])
        for o, tile in enumerate((s, 1 - s)):
            part = value[o * B : (o + 1) * B]
            out[tile] = part if total is None else part + refs[0][tile]

    return pl.pallas_call(
        kernel,
        in_specs=[SMEM, VMEM, HBM] + [VMEM] * (2 + len(totals)),
        out_specs=VMEM,
        out_shape=jax.ShapeDtypeStruct((2, B, 2 * B), F32),
        scratch_shapes=slab_scratch(even),
        input_output_aliases={5: 0} if totals else {},
        compiler_params=params(12),
        cost_estimate=cost(3 << 28, 2 << 20),
        name="multiply",
    )(place, sigma, other, even, odd, *totals)


N = 3 * B // 32


def along(y, core, sub):
    base = y if sub < 2 else y ^ SLOTS[core][2]
    other = base ^ SLOTS[core][1]
    return jnp.maximum(base, other) if sub % 2 else jnp.minimum(base, other)


def last_kernel(at, own, other, even, odd, total, weights, corner, pieces, whole, t_all, t_right, *scratch):
    x, y, s = at[2], at[1], at[3]
    value = slab_product(at, 4, own, other, even, odd, *scratch)
    for o, tile in enumerate((s, 1 - s)):
        t_all[tile] = total[tile] + value[o * B : (o + 1) * B]
    fill_right(t_right, 0, 0, t_all[...].reshape(2 * B, 2 * B))
    top = product(weights[:B], t_right[...])
    whole[:B] = top[:, :B]
    whole[B : 2 * B] = top[:, B:]
    whole[2 * B :] = product(weights[B:], t_right[:, B:])
    for core in range(2):
        for slot, apart in enumerate(SLOTS[core]):
            p = x ^ apart
            for sub in range(NY):
                start = (core * NX + p) * (NY * N) + along(y, core, sub) * N
                corner[core ^ s, slot, sub] = whole[pl.ds(pl.multiple_of(start, 8), N), :]
            rows = pl.ds(pl.multiple_of((p // 2 * 2 + core) * Q, 8), Q)
            pieces[core ^ s, slot] = t_all[lax.rem(p, 2), rows, :]


def last(place, sigma, other, even, odd, total, weights):
    return pl.pallas_call(
        last_kernel,
        in_specs=[SMEM, VMEM, HBM] + [VMEM] * 4,
        out_specs=[VMEM, VMEM],
        out_shape=[
            jax.ShapeDtypeStruct((2, NX, NY, N, B), F32),
            jax.ShapeDtypeStruct((2, NX, Q, 2 * B), F32),
        ],
        scratch_shapes=[
            pltpu.VMEM((3 * B, B), F32),
            pltpu.VMEM((2, B, 2 * B), F32),
            pltpu.VMEM((WIDE, 2 * B), BF16),
        ]
        + slab_scratch(even),
        compiler_params=params(20),
        cost_estimate=cost(1 << 30, 2 << 20),
        name="last",
    )(place, sigma, other, even, odd, total, weights)


def invert_kernel(_, one_ref, zero_ref, out_one, out_zero, one, zero, sems):
    copies = [pltpu.make_async_copy(one_ref, one, sems.at[0]), pltpu.make_async_copy(zero_ref, zero, sems.at[1])]
    for copy in copies:
        copy.start()
    for copy in copies:
        copy.wait()
    row = lax.broadcasted_iota(jnp.int32, (HALF, HALF), 0)
    col = lax.broadcasted_iota(jnp.int32, (HALF, HALF), 1)
    blocks, inverses = [], []
    for ref in (one, zero):
        for k in range(2):
            block = ref[k * HALF : (k + 1) * HALF, k * HALF : (k + 1) * HALF]
            blocks.append(block)
            inverses.append(jnp.where(row == col, 1.0 / block, 0.0))
    below = jnp.logical_and(row == col + 1, row % 2 == 1)
    scales = [jnp.sum(i, axis=1, keepdims=True) for i in inverses]
    inverses = [
        i - r * jnp.where(below, b, 0.0) * jnp.sum(i, axis=0, keepdims=True)
        for b, i, r in zip(blocks, inverses, scales)
    ]
    size = 2
    while size < HALF:
        below = jnp.logical_and(
            row // (2 * size) == col // (2 * size),
            jnp.logical_and((row // size) % 2 == 1, (col // size) % 2 == 0),
        )
        middles = [exact(jnp.where(below, b, 0.0), i) for b, i in zip(blocks, inverses)]
        inverses = [i - exact(i, m) for i, m in zip(inverses, middles)]
        size *= 2
    for n, (ref, out) in enumerate(((one, out_one), (zero, out_zero))):
        top, bottom = inverses[2 * n], inverses[2 * n + 1]
        out[:HALF, :HALF] = top
        out[HALF:, HALF:] = bottom
        out[:HALF, HALF:] = jnp.zeros((HALF, HALF), F32)
        out[HALF:, :HALF] = -exact(bottom, exact(ref[HALF:, :HALF], top))


def invert(place, one, zero):
    tile = jax.ShapeDtypeStruct((B, B), F32)
    return pl.pallas_call(
        invert_kernel,
        in_specs=[SMEM, HBM, HBM],
        out_specs=[VMEM, VMEM],
        out_shape=[tile, tile],
        scratch_shapes=[pltpu.VMEM((B, B), F32), pltpu.VMEM((B, B), F32), pltpu.SemaphoreType.DMA((2,))],
        compiler_params=params(),
        cost_estimate=cost(1 << 32, 1 << 20),
        name="invert",
    )(place, one, zero)


def constants_kernel(x1_ref, x0_ref, link, z_terms, zt_terms, base):
    x1, x0 = x1_ref[...], x0_ref[...]
    hl = dot3(link[...], x0, NN)
    top = -dot3(x1, hl, NN)
    none = jnp.zeros((B, B), F32)
    for row, column, block in ((0, 0, x1), (0, B, top), (B, 0, none), (B, B, x0)):
        fill_right(z_terms, row, column, block)
        fill_left(zt_terms, column, row, block.T)
    inv1 = dot3(x1, x1, TN)
    cross = dot3(inv1, hl, NN)
    base[:B] = inv1
    base[B : 2 * B] = -cross
    base[2 * B :] = dot3(x0, x0, TN) + dot3(hl, cross, TN)


def constants(x1, x0, link):
    return pl.pallas_call(
        constants_kernel,
        in_specs=[VMEM] * 3,
        out_specs=[VMEM] * 3,
        out_shape=[
            jax.ShapeDtypeStruct((WIDE, 2 * B), BF16),
            jax.ShapeDtypeStruct((2 * B, WIDE), BF16),
            jax.ShapeDtypeStruct((3 * B, B), F32),
        ],
        compiler_params=params(),
        cost_estimate=cost(1 << 29, 3 << 20),
        name="constants",
    )(x1, x0, link)


def weigh_kernel(at, mine, others, weights, rows):
    x, y, s = at[2], at[1], at[3]
    for tile in range(2):
        for g in range(2):
            for core in range(2):
                near = (tile ^ lax.rem(x, 2)) * 2 + (g ^ lax.rem(y, 2))
                start = ((tile * 2 + g) * 2 + core) * Q
                for panel in range(2):
                    block = jnp.where(s == core, mine[near, panel], others[near, panel])
                    rows[start : start + Q, panel * B : (panel + 1) * B] = block
    fill_left(weights, 0, 0, rows[...].T)


def weigh(place, mine, others):
    return pl.pallas_call(
        weigh_kernel,
        in_specs=[SMEM] + [VMEM] * 2,
        out_specs=VMEM,
        out_shape=jax.ShapeDtypeStruct((2 * B, WIDE), BF16),
        scratch_shapes=[pltpu.VMEM((2 * B, 2 * B), F32)],
        compiler_params=params(),
        cost_estimate=cost(1 << 28, 3 << 20),
        name="weigh",
    )(place, mine, others)


def rows_kernel(a, b, z_terms, s1, s0, left):
    fill_left(left, 0, 0, a[...] + b[...])
    both = product(left[...], z_terms[...])
    s1[...] = -both[:, :B]
    s0[...] = -both[:, B:]


def rows(a, b, z_terms):
    out = jax.ShapeDtypeStruct((Q, B), F32)
    return pl.pallas_call(
        rows_kernel,
        in_specs=[VMEM] * 3,
        out_specs=[VMEM] * 2,
        out_shape=[out, out],
        scratch_shapes=[pltpu.VMEM((Q, WIDE), BF16)],
        compiler_params=params(),
        cost_estimate=cost(1 << 27, 2 << 20),
        name="rows",
    )(a, b, z_terms)


def finish_kernel(at, mine, other, z_terms, zt_terms, base, s11, s10, s00, whole, left, right):
    x, y, s = at[2], at[1], at[3]
    for core in range(2):

        def place_all(ref):
            for slot, apart in enumerate(SLOTS[core]):
                for sub in range(NY):
                    start = (core * NX + (x ^ apart)) * (NY * N) + along(y, core, sub) * N
                    whole[pl.ds(pl.multiple_of(start, 8), N), :] = ref[slot, sub // 2, sub % 2]

        @pl.when(s == core)
        def _():
            place_all(mine)

        @pl.when(s != core)
        def _():
            place_all(other)

    crossed = whole[B : 2 * B]
    fill_left(left, 0, 0, whole[:B])
    fill_left(left, 0, B, crossed)
    fill_left(left, B, 0, crossed.T)
    fill_left(left, B, B, whole[2 * B :])
    fill_right(right, 0, 0, half_product(left, z_terms, slice(0, B)))
    fill_right(right, 0, B, product(left[...], z_terms[:, B:]))
    top = half_product(zt_terms, right, slice(0, 2 * B))
    s11[...] = top[:, :B] + base[:B]
    s10[...] = top[:, B:] + base[B : 2 * B]
    s00[...] = product(zt_terms[B:], right[:, B:]) + base[2 * B :]


def finish(place, mine, other, z_terms, zt_terms, base):
    tile = jax.ShapeDtypeStruct((B, B), F32)
    return pl.pallas_call(
        finish_kernel,
        in_specs=[SMEM] + [VMEM] * 5,
        out_specs=[VMEM] * 3,
        out_shape=[tile, tile, tile],
        scratch_shapes=[
            pltpu.VMEM((3 * B, B), F32),
            pltpu.VMEM((2 * B, WIDE), BF16),
            pltpu.VMEM((WIDE, 2 * B), BF16),
        ],
        compiler_params=params(),
        cost_estimate=cost(1 << 28, 3 << 20),
        name="finish",
    )(place, mine, other, z_terms, zt_terms, base)


def body(sigma, p1, p0, link, diag_one, diag_zero):
    x, y, z, s = (lax.axis_index(name).astype(jnp.int32) for name in ("x", "y", "z", "s"))
    way = 2 * s - 1
    place = jnp.stack([z, y, x, s] + [lax.rem(z + NZ + j * way, NZ) for j in range(5)])

    view = (NZ,) + SLAB
    own = jnp.stack([p1, p0])[None]
    a = jnp.concatenate([own, to_core(own)], axis=0)
    y2 = send(own, lambda x, y, z, s: (x, y + 2, z, s))
    a1 = along_z(a)
    staged = stage(after(place, a), sigma.reshape(view))
    y2 = after(y2, a, *staged)
    b = jnp.concatenate([y2, to_core(y2)], axis=0)
    b1 = along_z(b)
    a2 = along_z(after(a1, b))

    sigma_other = to_core(after(sigma, b, a1)).reshape(view)
    even = jnp.concatenate([own, after(y2, a1)], axis=0)
    odd = along_y(even)
    b1, odd = after((b1, odd), b1, odd)
    b2 = along_z(b1)
    z1 = jnp.concatenate([a1, b1], axis=0)
    e1 = along_y(z1)
    pair = jnp.concatenate([own, jnp.where(y % 2 == s, odd[1:], odd[:1])], axis=0)
    a3 = along_z(after(a2, b1))
    crossed = send(after(pair, a2), lambda x, y, z, s: (x ^ 2, y, z, s))

    b2 = after(b2, a2)
    b3 = along_z(b2)
    z2 = jnp.concatenate([a2, b2], axis=0)
    e2 = along_y(z2)
    a3 = after(a3, b2)
    total = multiply(place, 0, staged[0], sigma_other, even, odd)

    b3, crossed = after((b3, crossed), b3, crossed, a3, total)
    z4 = along_z(jnp.concatenate([a3[:1], b3[:1]], axis=0))
    z3 = jnp.concatenate([a3, b3], axis=0)
    e3 = along_y(z3)
    first = jnp.where(x // 2 == y % 2, pair, crossed)
    second = send(first, lambda x, y, z, s: (x ^ 1, y, z, s))
    total = multiply(place, 1, staged[1], sigma_other, z1, e1, total)

    z4, second, e2 = after((z4, second, e2), z4, second, e2, total)
    e4 = along_y(z4)
    mine = jnp.concatenate([first, second], axis=0)
    others = to_core(mine)
    total = multiply(place, 2, staged[2], sigma_other, z2, e2, total)
    weights = weigh(place, mine, others)
    total = multiply(place, 3, staged[3], sigma_other, z3, e3, total)
    corner, pieces = last(place, staged[4], sigma_other, z4, e4, total, weights)

    part = corner[0] + to_core(corner[1])
    came = swap(part[2:], "x", 0)
    q = pieces[0] + to_core(pieces[1])
    x1, x0 = invert(after(place, part), diag_one, diag_zero)
    part = part[:2] + after(came, x1, x0, q)
    part = part.reshape(2, 2, 2, N, B)
    a, b, c = to_second_x(part[1, 0]), to_first_y(part[0, 1]), to_both(part[1, 1])
    z_terms, zt_terms, base = constants(x1, x0, after(link, part))
    part = (part[0, 0] + after(a, base)) + (b + c)
    got = swap(q[2:], "x", 0)
    a, b, c = swap(part, "y", 1), to_pair(part, 1), to_pair_y(after(part, got))
    q = q[:2] + got
    part = (part + a) + (b + c)
    got = swap(q[1], "x", 1)
    a, b, c = to_pair(part, 2), to_pair(part, 4), to_pair(after(part, got), 6)
    part = (part + a) + (b + c)
    s1, s0 = rows(q[0], got, z_terms)
    sigmas = send(jnp.stack([s1, s0]), lambda x, y, z, s: (y % 2 * 2 + x % 2, y // 2 * 2 + x // 2, z, s))
    a, b, c = to_second_x(part), to_first_y(part), to_both(after(part, sigmas))
    part = jnp.stack([jnp.stack([part, b]), jnp.stack([a, c])])
    mine = jnp.concatenate([part, swap(part, "x", 0)], axis=0)
    s11, s10, s00 = finish(place, mine, to_core(mine), z_terms, zt_terms, base)
    return sigmas[0], s11, sigmas[1], s10, s00


def solution(mesh):
    mesh = Mesh(mesh.devices.reshape(NX, NZ, NY, 2), AXES)
    in_specs = (P("x", AXES[1:]), P(AXES, None), P(AXES, None), P(), P(), P())
    out_specs = (P(AXES, None), P(), P(AXES, None), P(), P())
    return jax.shard_map(body, mesh=mesh, in_specs=in_specs, out_specs=out_specs, check_vma=False)
```

```python
import jax
import jax.numpy as jnp
from jax import lax
from jax.experimental import pallas as pl
from jax.experimental.pallas import tpu as pltpu
from jax.sharding import Mesh, PartitionSpec as P

F32 = jnp.float32
BF16 = jnp.bfloat16
AXES = ("x", "z", "y", "s")
NX, NY, NZ = 4, 4, 8
B = 256
Q = 64
HALF = 128


def device(x, y, z, s):
    return (x % NX) * 64 + (z % NZ) * 8 + (y % NY) * 2 + s


def send(block, move):
    pairs = [
        (device(x, y, z, s), device(*move(x, y, z, s)))
        for x in range(NX)
        for z in range(NZ)
        for y in range(NY)
        for s in range(2)
    ]
    return lax.ppermute(block, AXES, pairs)


def to_core(block):
    return send(block, lambda x, y, z, s: (x, y, z, 1 - s))


def along_y(block):
    return send(block, lambda x, y, z, s: (x, y + 1 - 2 * s, z, s))


def along_z(block):
    return send(block, lambda x, y, z, s: (x, y, z + 1 - 2 * s, s))


SLOTS = ((0, 3, 1, 2), (0, 1, 3, 2))


def swap(block, axis, turn):
    def move(x, y, z, s):
        apart = SLOTS[s][2 - turn]
        return (x ^ apart, y, z, s) if axis == "x" else (x, y ^ apart, z, s)

    return send(block, move)


def to_pair(block, far):
    return send(block, lambda x, y, z, s: (x, y, ((z + NZ - s) % NZ ^ far) + s, s))


def to_pair_y(block):
    return send(block, lambda x, y, z, s: (x, y ^ SLOTS[s][1], ((z + NZ - s) % NZ ^ 1) + s, s))


def to_second_x(block):
    return swap(block, "x", 1)


def to_first_y(block):
    return swap(block, "y", 0)


def to_both(block):
    return send(block, lambda x, y, z, s: (x ^ SLOTS[s][1], y ^ SLOTS[s][2], z, s))


def after(value, *earlier):
    return lax.optimization_barrier((value, earlier))[0]


def split(value):
    high = value.astype(BF16)
    return high, (value - high.astype(F32)).astype(BF16)


def dot3(left, right, dims):
    lh, ll = split(left)
    rh, rl = split(right)
    d = (dims, ((), ()))
    out = lax.dot_general(lh, rh, d, preferred_element_type=F32)
    out += lax.dot_general(ll, rh, d, preferred_element_type=F32)
    return out + lax.dot_general(lh, rl, d, preferred_element_type=F32)


NN = ((1,), (0,))
TN = ((0,), (0,))


def fill_left(ref, row, place, value):
    deep = ref.shape[1] // 3
    high, low = split(value)
    m, k = value.shape
    ref[row : row + m, place : place + k] = high
    ref[row : row + m, deep + place : deep + place + k] = low
    ref[row : row + m, 2 * deep + place : 2 * deep + place + k] = high


def fill_right(ref, place, column, value):
    deep = ref.shape[0] // 3
    high, low = split(value)
    k, n = value.shape
    ref[place : place + k, column : column + n] = high
    ref[deep + place : deep + place + k, column : column + n] = high
    ref[2 * deep + place : 2 * deep + place + k, column : column + n] = low


def product(left, right):
    return jnp.dot(left, right, preferred_element_type=F32)


def exact(left, right):
    return jnp.dot(left, right, precision=lax.Precision.HIGHEST, preferred_element_type=F32)


def params(limit=16):
    return pltpu.CompilerParams(vmem_limit_bytes=limit * 1024 * 1024)


def cost(flops, moved):
    return pl.CostEstimate(flops=flops, bytes_accessed=moved, transcendentals=0)


VMEM = pl.BlockSpec(memory_space=pltpu.VMEM)
SMEM = pl.BlockSpec(memory_space=pltpu.SMEM)
HBM = pl.BlockSpec(memory_space=pltpu.HBM)
WIDE = 6 * B
SLAB = (NY, 2, Q, B)


def stage(place, sigma):
    def kernel(at, ref, out, sems):
        copies = [pltpu.make_async_copy(ref.at[at[4 + n]], out.at[n], sems.at[n]) for n in range(5)]
        for copy in copies:
            copy.start()
        for copy in copies:
            copy.wait()

    return pl.pallas_call(
        kernel,
        in_specs=[SMEM, HBM],
        out_specs=VMEM,
        out_shape=jax.ShapeDtypeStruct((5,) + SLAB, F32),
        scratch_shapes=[pltpu.SemaphoreType.DMA((5,))],
        compiler_params=params(),
        cost_estimate=cost(0, 5 << 20),
        name="stage",
    )(place, sigma)


def slab_product(at, step, own, other, even, odd, left, right, slabs, sems):
    y, s, slab = at[1], at[3], at[4 + step]
    copy = pltpu.make_async_copy(other.at[slab], slabs, sems.at[0])
    copy.start()
    depth = even.shape[0] * Q
    for n, ref in enumerate((even, odd)):
        for panel in range(2):
            fill_right(right, n * depth, panel * B, ref[:, panel].reshape(depth, B))
    near = lax.rem(y + 3 + 2 * s, NY)
    for o in range(2):
        if o == 1:
            copy.wait()
        for n, first in enumerate((y, near)):
            blocks = [
                (slabs if o else own.at[step])[lax.rem(first + 2 * d, NY), core]
                for d in range(2)
                for core in (s, 1 - s)[: depth // 128]
            ]
            fill_left(left, o * B, n * depth, jnp.concatenate(blocks, axis=0).T)
    return product(left[...], right[...])


def slab_scratch(even):
    deep = 6 * even.shape[0] * Q
    return [
        pltpu.VMEM((2 * B, deep), BF16),
        pltpu.VMEM((deep, 2 * B), BF16),
        pltpu.VMEM(SLAB, F32),
        pltpu.SemaphoreType.DMA((1,)),
    ]


def multiply(place, step, sigma, other, even, odd, total=None):
    totals = [] if total is None else [total]

    def kernel(at, own_ref, other_ref, even_ref, odd_ref, *refs):
        s = at[3]
        out = refs[len(totals)]
        value = slab_product(at, step, own_ref, other_ref, even_ref, odd_ref, *refs[len(totals) + 1 :])
        for o, tile in enumerate((s, 1 - s)):
            part = value[o * B : (o + 1) * B]
            out[tile] = part if total is None else part + refs[0][tile]

    return pl.pallas_call(
        kernel,
        in_specs=[SMEM, VMEM, HBM] + [VMEM] * (2 + len(totals)),
        out_specs=VMEM,
        out_shape=jax.ShapeDtypeStruct((2, B, 2 * B), F32),
        scratch_shapes=slab_scratch(even),
        input_output_aliases={5: 0} if totals else {},
        compiler_params=params(30),
        cost_estimate=cost(3 << 28, 2 << 20),
        name="multiply",
    )(place, sigma, other, even, odd, *totals)


N = 3 * B // 32


def along(y, core, sub):
    base = y if sub < 2 else y ^ SLOTS[core][2]
    other = base ^ SLOTS[core][1]
    return jnp.maximum(base, other) if sub % 2 else jnp.minimum(base, other)


def last_kernel(at, own, other, even, odd, total, weights, corner, pieces, whole, t_all, t_right, *scratch):
    x, y, s = at[2], at[1], at[3]
    value = slab_product(at, 4, own, other, even, odd, *scratch)
    for o, tile in enumerate((s, 1 - s)):
        t_all[tile] = total[tile] + value[o * B : (o + 1) * B]
    fill_right(t_right, 0, 0, t_all[...].reshape(2 * B, 2 * B))
    top = product(weights[:B], t_right[...])
    whole[:B] = top[:, :B]
    whole[B : 2 * B] = top[:, B:]
    whole[2 * B :] = product(weights[B:], t_right[:, B:])
    for core in range(2):
        for slot, apart in enumerate(SLOTS[core]):
            p = x ^ apart
            for sub in range(NY):
                start = (core * NX + p) * (NY * N) + along(y, core, sub) * N
                corner[core ^ s, slot, sub] = whole[pl.ds(pl.multiple_of(start, 8), N), :]
            rows = pl.ds(pl.multiple_of((p // 2 * 2 + core) * Q, 8), Q)
            pieces[core ^ s, slot] = t_all[lax.rem(p, 2), rows, :]


def last(place, sigma, other, even, odd, total, weights):
    return pl.pallas_call(
        last_kernel,
        in_specs=[SMEM, VMEM, HBM] + [VMEM] * 4,
        out_specs=[VMEM, VMEM],
        out_shape=[
            jax.ShapeDtypeStruct((2, NX, NY, N, B), F32),
            jax.ShapeDtypeStruct((2, NX, Q, 2 * B), F32),
        ],
        scratch_shapes=[
            pltpu.VMEM((3 * B, B), F32),
            pltpu.VMEM((2, B, 2 * B), F32),
            pltpu.VMEM((WIDE, 2 * B), BF16),
        ]
        + slab_scratch(even),
        compiler_params=params(30),
        cost_estimate=cost(1 << 30, 2 << 20),
        name="last",
    )(place, sigma, other, even, odd, total, weights)


def invert_kernel(_, one_ref, zero_ref, out_one, out_zero, one, zero, sems):
    copies = [pltpu.make_async_copy(one_ref, one, sems.at[0]), pltpu.make_async_copy(zero_ref, zero, sems.at[1])]
    for copy in copies:
        copy.start()
    for copy in copies:
        copy.wait()
    row = lax.broadcasted_iota(jnp.int32, (HALF, HALF), 0)
    col = lax.broadcasted_iota(jnp.int32, (HALF, HALF), 1)
    blocks, inverses = [], []
    for ref in (one, zero):
        for k in range(2):
            block = ref[k * HALF : (k + 1) * HALF, k * HALF : (k + 1) * HALF]
            blocks.append(block)
            inverses.append(jnp.where(row == col, 1.0 / block, 0.0))
    below = jnp.logical_and(row == col + 1, row % 2 == 1)
    scales = [jnp.sum(i, axis=1, keepdims=True) for i in inverses]
    inverses = [
        i - r * jnp.where(below, b, 0.0) * jnp.sum(i, axis=0, keepdims=True)
        for b, i, r in zip(blocks, inverses, scales)
    ]
    size = 2
    while size < HALF:
        below = jnp.logical_and(
            row // (2 * size) == col // (2 * size),
            jnp.logical_and((row // size) % 2 == 1, (col // size) % 2 == 0),
        )
        middles = [exact(jnp.where(below, b, 0.0), i) for b, i in zip(blocks, inverses)]
        inverses = [i - exact(i, m) for i, m in zip(inverses, middles)]
        size *= 2
    for n, (ref, out) in enumerate(((one, out_one), (zero, out_zero))):
        top, bottom = inverses[2 * n], inverses[2 * n + 1]
        out[:HALF, :HALF] = top
        out[HALF:, HALF:] = bottom
        out[:HALF, HALF:] = jnp.zeros((HALF, HALF), F32)
        out[HALF:, :HALF] = -exact(bottom, exact(ref[HALF:, :HALF], top))


def invert(place, one, zero):
    tile = jax.ShapeDtypeStruct((B, B), F32)
    return pl.pallas_call(
        invert_kernel,
        in_specs=[SMEM, HBM, HBM],
        out_specs=[VMEM, VMEM],
        out_shape=[tile, tile],
        scratch_shapes=[pltpu.VMEM((B, B), F32), pltpu.VMEM((B, B), F32), pltpu.SemaphoreType.DMA((2,))],
        compiler_params=params(),
        cost_estimate=cost(1 << 32, 1 << 20),
        name="invert",
    )(place, one, zero)


def constants_kernel(x1_ref, x0_ref, link, z_terms, zt_terms, base):
    x1, x0 = x1_ref[...], x0_ref[...]
    hl = dot3(link[...], x0, NN)
    top = -dot3(x1, hl, NN)
    none = jnp.zeros((B, B), F32)
    for row, column, block in ((0, 0, x1), (0, B, top), (B, 0, none), (B, B, x0)):
        fill_right(z_terms, row, column, block)
        fill_left(zt_terms, column, row, block.T)
    inv1 = dot3(x1, x1, TN)
    cross = dot3(inv1, hl, NN)
    base[:B] = inv1
    base[B : 2 * B] = -cross
    base[2 * B :] = dot3(x0, x0, TN) + dot3(hl, cross, TN)


def constants(x1, x0, link):
    return pl.pallas_call(
        constants_kernel,
        in_specs=[VMEM] * 3,
        out_specs=[VMEM] * 3,
        out_shape=[
            jax.ShapeDtypeStruct((WIDE, 2 * B), BF16),
            jax.ShapeDtypeStruct((2 * B, WIDE), BF16),
            jax.ShapeDtypeStruct((3 * B, B), F32),
        ],
        compiler_params=params(),
        cost_estimate=cost(1 << 29, 3 << 20),
        name="constants",
    )(x1, x0, link)


def weigh_kernel(at, mine, others, weights, rows):
    x, y, s = at[2], at[1], at[3]
    for tile in range(2):
        for g in range(2):
            for core in range(2):
                near = (tile ^ lax.rem(x, 2)) * 2 + (g ^ lax.rem(y, 2))
                start = ((tile * 2 + g) * 2 + core) * Q
                for panel in range(2):
                    block = jnp.where(s == core, mine[near, panel], others[near, panel])
                    rows[start : start + Q, panel * B : (panel + 1) * B] = block
    fill_left(weights, 0, 0, rows[...].T)


def weigh(place, mine, others):
    return pl.pallas_call(
        weigh_kernel,
        in_specs=[SMEM] + [VMEM] * 2,
        out_specs=VMEM,
        out_shape=jax.ShapeDtypeStruct((2 * B, WIDE), BF16),
        scratch_shapes=[pltpu.VMEM((2 * B, 2 * B), F32)],
        compiler_params=params(),
        cost_estimate=cost(1 << 28, 3 << 20),
        name="weigh",
    )(place, mine, others)


def rows_kernel(a, b, z_terms, s1, s0, left):
    fill_left(left, 0, 0, a[...] + b[...])
    both = product(left[...], z_terms[...])
    s1[...] = -both[:, :B]
    s0[...] = -both[:, B:]


def rows(a, b, z_terms):
    out = jax.ShapeDtypeStruct((Q, B), F32)
    return pl.pallas_call(
        rows_kernel,
        in_specs=[VMEM] * 3,
        out_specs=[VMEM] * 2,
        out_shape=[out, out],
        scratch_shapes=[pltpu.VMEM((Q, WIDE), BF16)],
        compiler_params=params(),
        cost_estimate=cost(1 << 27, 2 << 20),
        name="rows",
    )(a, b, z_terms)


def finish_kernel(at, mine, other, z_terms, zt_terms, base, s11, s10, s00, whole, left, right):
    x, y, s = at[2], at[1], at[3]
    for core in range(2):

        def place_all(ref):
            for slot, apart in enumerate(SLOTS[core]):
                for sub in range(NY):
                    start = (core * NX + (x ^ apart)) * (NY * N) + along(y, core, sub) * N
                    whole[pl.ds(pl.multiple_of(start, 8), N), :] = ref[slot, sub // 2, sub % 2]

        @pl.when(s == core)
        def _():
            place_all(mine)

        @pl.when(s != core)
        def _():
            place_all(other)

    crossed = whole[B : 2 * B]
    fill_left(left, 0, 0, whole[:B])
    fill_left(left, 0, B, crossed)
    fill_left(left, B, 0, crossed.T)
    fill_left(left, B, B, whole[2 * B :])
    fill_right(right, 0, 0, product(left[...], z_terms[...]))
    top = product(zt_terms[:B], right[...])
    s11[...] = top[:, :B] + base[:B]
    s10[...] = top[:, B:] + base[B : 2 * B]
    s00[...] = product(zt_terms[B:], right[:, B:]) + base[2 * B :]


def finish(place, mine, other, z_terms, zt_terms, base):
    tile = jax.ShapeDtypeStruct((B, B), F32)
    return pl.pallas_call(
        finish_kernel,
        in_specs=[SMEM] + [VMEM] * 5,
        out_specs=[VMEM] * 3,
        out_shape=[tile, tile, tile],
        scratch_shapes=[
            pltpu.VMEM((3 * B, B), F32),
            pltpu.VMEM((2 * B, WIDE), BF16),
            pltpu.VMEM((WIDE, 2 * B), BF16),
        ],
        compiler_params=params(),
        cost_estimate=cost(1 << 28, 3 << 20),
        name="finish",
    )(place, mine, other, z_terms, zt_terms, base)


def body(sigma, p1, p0, link, diag_one, diag_zero):
    x, y, z, s = (lax.axis_index(name).astype(jnp.int32) for name in ("x", "y", "z", "s"))
    way = 2 * s - 1
    place = jnp.stack([z, y, x, s] + [lax.rem(z + NZ + j * way, NZ) for j in range(5)])

    view = (NZ,) + SLAB
    own = jnp.stack([p1, p0])[None]
    a = jnp.concatenate([own, to_core(own)], axis=0)
    y2 = send(own, lambda x, y, z, s: (x, y + 2, z, s))
    a1 = along_z(a)
    staged = stage(after(place, a), sigma.reshape(view))
    y2 = after(y2, a, staged)
    b = jnp.concatenate([y2, to_core(y2)], axis=0)
    b1 = along_z(b)
    a2 = along_z(after(a1, b))

    sigma_other = to_core(after(sigma, b, a1)).reshape(view)
    even = jnp.concatenate([own, after(y2, a1)], axis=0)
    odd = along_y(even)
    x1, x0 = invert(after(place, b, a1), diag_one, diag_zero)
    b1, odd = after((b1, odd), b1, odd, x1, x0)
    b2 = along_z(b1)
    z1 = jnp.concatenate([a1, b1], axis=0)
    e1 = along_y(z1)
    pair = jnp.concatenate([own, jnp.where(y % 2 == s, odd[1:], odd[:1])], axis=0)
    a3 = along_z(after(a2, b1))
    crossed = send(after(pair, a2), lambda x, y, z, s: (x ^ 2, y, z, s))

    b2 = after(b2, a2)
    b3 = along_z(b2)
    z2 = jnp.concatenate([a2, b2], axis=0)
    e2 = along_y(z2)
    a3 = after(a3, b2)
    total = multiply(place, 0, staged, sigma_other, even, odd)

    b3, crossed = after((b3, crossed), b3, crossed, a3, total)
    z4 = along_z(jnp.concatenate([a3[:1], b3[:1]], axis=0))
    z3 = jnp.concatenate([a3, b3], axis=0)
    e3 = along_y(z3)
    first = jnp.where(x // 2 == y % 2, pair, crossed)
    second = send(first, lambda x, y, z, s: (x ^ 1, y, z, s))
    total = multiply(place, 1, staged, sigma_other, z1, e1, total)

    z4, second, e2 = after((z4, second, e2), z4, second, e2, total)
    e4 = along_y(z4)
    mine = jnp.concatenate([first, second], axis=0)
    others = to_core(mine)
    total = multiply(place, 2, staged, sigma_other, z2, e2, total)
    weights = weigh(place, mine, others)
    total = multiply(place, 3, staged, sigma_other, z3, e3, total)
    corner, pieces = last(place, staged, sigma_other, z4, e4, total, weights)

    part = corner[0] + to_core(corner[1])
    came = swap(part[2:], "x", 0)
    q = pieces[0] + to_core(pieces[1])
    part = part[:2] + after(came, q)
    part = part.reshape(2, 2, 2, N, B)
    a, b, c = to_second_x(part[1, 0]), to_first_y(part[0, 1]), to_both(part[1, 1])
    z_terms, zt_terms, base = constants(x1, x0, after(link, part))
    part = (part[0, 0] + after(a, base)) + (b + c)
    got = swap(q[2:], "x", 0)
    a, b, c = swap(part, "y", 1), to_pair(part, 1), to_pair_y(after(part, got))
    q = q[:2] + got
    part = (part + a) + (b + c)
    got = swap(q[1], "x", 1)
    a, b, c = to_pair(part, 2), to_pair(part, 4), to_pair(after(part, got), 6)
    part = (part + a) + (b + c)
    s1, s0 = rows(q[0], got, z_terms)
    sigmas = send(jnp.stack([s1, s0]), lambda x, y, z, s: (y % 2 * 2 + x % 2, y // 2 * 2 + x // 2, z, s))
    a, b, c = to_second_x(part), to_first_y(part), to_both(after(part, sigmas))
    part = jnp.stack([jnp.stack([part, b]), jnp.stack([a, c])])
    mine = jnp.concatenate([part, swap(part, "x", 0)], axis=0)
    s11, s10, s00 = finish(place, mine, to_core(mine), z_terms, zt_terms, base)
    return sigmas[0], s11, sigmas[1], s10, s00


def solution(mesh):
    mesh = Mesh(mesh.devices.reshape(NX, NZ, NY, 2), AXES)
    in_specs = (P("x", AXES[1:]), P(AXES, None), P(AXES, None), P(), P(), P())
    out_specs = (P(AXES, None), P(), P(AXES, None), P(), P())
    return jax.shard_map(body, mesh=mesh, in_specs=in_specs, out_specs=out_specs, check_vma=False)
```
